32 devices in a mesh: gx: 16 (over z, y, core), gy: 2 (over x).
Axes of the slice: x: 2, y: 2, z: 4, core: 2. Of those that a mesh axis runs over, the one named last changes fastest.
Arguments:
- embed: bfloat16 [32, 8, 128, 128], P('gx', 'gy')
- frac: bfloat16 [32, 8, 3, 128], P('gx', 'gy'), may hold values from 0 to 1
- pair_blocks: int32 [32, 8, 5], P('gx', 'gy'), may hold values from 0 to 8, as said below
- w_in: bfloat16 [128, 128], replicated, may hold values from -0.5 to 0.5
- rbf_mix: float32 [8, 128], replicated, may hold values from -4 to 4
- w_charge: bfloat16 [128, 128], replicated, may hold values from -0.5 to 0.5
- k_index: int32 [3, 512], replicated, may hold values from -8 to 8
- k_weight: float32 [512], replicated, may hold values from 0.2 to 2
Outputs:
- updated: float32 [32, 8, 128, 128], P('gx', 'gy')
The draws below stay inside these ranges and needn't reach their ends.
Inputs may be any that keep to these rules, and one draw needn't show every extreme that they name: `pair_blocks`: for every column, 5 different codes 3 * (dx + 1) + (dy + 1) of columns at offsets dx, dy in -1, 0, 1 along the first two dimensions; the first code is 4, the column itself, the others name other columns.
All inputs are finite; a program needn't handle non-finite values.
Results may differ from the reference program's by a relative error of at most 0.002.
Values may be sent and summed in bfloat16 or wider, within the bound.
No kernel may reach another device: no remote copies, remote signals or barrier semaphores. Data moves between devices by JAX's collectives and lax.ppermute only.
A program may use at most 64 MiB of HBM per device.

```python
import math
import jax
import jax.numpy as jnp
from jax import lax

HID = 128
KVEC = 512
NRBF = 8
ATOMS_BLK = 128
NPB = 5
NBX = 32
NBY = 8
ATOMS = 32768


def draw_pair_blocks(key, part):
    key = jax.random.fold_in(key, 11)
    scores = jax.random.randint(key, (NBX, NBY, 8), 0, 1 << 20) * 8 + jnp.arange(8, dtype=jnp.int32)
    picked = jnp.argsort(scores, axis=-1)[..., :NPB - 1].astype(jnp.int32)
    others = picked + (picked >= 4).astype(jnp.int32)
    itself = jnp.full((NBX, NBY, 1), 4, jnp.int32)
    return jnp.concatenate([itself, others], axis=-1).astype(jnp.int32)


def draw_embed(key, part):
    key = jax.random.fold_in(key, 5)
    key_base, key_mean = jax.random.split(key, 2)
    mean_vec = jax.random.normal(key_mean, (HID,), jnp.float32)
    ramp = jnp.arange(NBX, dtype=jnp.float32) / NBX
    base = jax.random.normal(key_base, (NBX, NBY, ATOMS_BLK, HID), jnp.float32)
    level = 0.2 + 1.2 * ramp
    values = base + mean_vec[None, None, None, :] * level[:, None, None, None]
    return values.astype(jnp.bfloat16)


def touch_ends(entries, own_key, smallest, high):
    extent = entries.shape
    place = [jax.random.randint(jax.random.fold_in(own_key, axis), (), 0, extent[axis]) for axis in range(len(extent))]
    entries = entries.at[tuple(place)].set(smallest)
    longest = extent.index(max(extent))
    place[longest] = (place[longest] + 1) % extent[longest]
    return entries.at[tuple(place)].set(high)


def levels(stream_key, extent, shards, smallest, largest):
    gain, own = 1.0, jax.random.fold_in(stream_key, 6)
    for position, shards_of in shards:
        draws = jnp.exp(jax.random.uniform(jax.random.fold_in(own, position), (shards_of,), jnp.float32, smallest / len(shards), largest / len(shards)))
        gain = gain * jnp.repeat(draws, extent[position] // shards_of).reshape([-1 if axis == position else 1 for axis in range(len(extent))])
    return gain


def normal_values(key, shape, width, most, held_as=jnp.bfloat16):
    values = width * jax.random.normal(key, shape, jnp.float32)
    return jnp.clip(values, min=-most, max=most).astype(held_as)


def setup_inputs(seed: int = 0) -> dict:
    arg_keys = jax.random.split(jax.random.key(seed), 9)
    return {
        "embed": draw_embed(jax.random.fold_in(arg_keys[8], 71), 0),
        "frac": jnp.clip(1.0 * jax.random.uniform(arg_keys[1], (NBX, NBY, 3, ATOMS_BLK), jnp.float32) ** levels(arg_keys[1], (NBX, NBY, 3, ATOMS_BLK), ((0, 16), (1, 2)), -0.2, 0.2), 0.0, 1.0).astype(jnp.bfloat16),
        "pair_blocks": draw_pair_blocks(jax.random.fold_in(arg_keys[8], 71), 0),
        "w_in": normal_values(arg_keys[3], (HID, HID), HID ** -0.5, 0.5),
        "rbf_mix": normal_values(arg_keys[4], (NRBF, HID), 1.0, 4.0, jnp.float32),
        "w_charge": normal_values(arg_keys[5], (HID, HID), HID ** -0.5, 0.5),
        "k_index": touch_ends(jax.random.randint(arg_keys[6], (3, KVEC), -8, 9), jax.random.fold_in(arg_keys[6], 1), -8, 8).astype(jnp.int32),
        "k_weight": jnp.clip(jnp.exp(jax.random.uniform(arg_keys[7], (KVEC,), jnp.float32, math.log(0.2), math.log(2.0))), 0.2, 2.0),
    }


CELL = 5.0
HEIGHT = 51.2
CUTOFF = 5.0
MSG_SCALE = 0.5

def pair_messages(own_f, nbr_f, nbr_x, shift_x, shift_y, rbf_mix):
    delta_x = (nbr_f[:, 0, None, :] + shift_x[:, None, None] - own_f[0][None, :, None]) * CELL
    delta_y = (nbr_f[:, 1, None, :] + shift_y[:, None, None] - own_f[1][None, :, None]) * CELL
    delta_z = (nbr_f[:, 2, None, :] - own_f[2][None, :, None]) * HEIGHT
    delta_z = jnp.where(delta_z > 0.5 * HEIGHT, delta_z - HEIGHT, jnp.where(delta_z < -0.5 * HEIGHT, delta_z + HEIGHT, delta_z))
    distance = jnp.sqrt(delta_x * delta_x + delta_y * delta_y + delta_z * delta_z)
    envelope = 0.5 * (jnp.cos(jnp.pi * jnp.minimum(distance, CUTOFF) / CUTOFF) + 1.0)
    basis_count = rbf_mix.shape[0]
    centers = jnp.arange(basis_count, dtype=jnp.float32) * (CUTOFF / (basis_count - 1))
    sharpness = ((basis_count - 1) / CUTOFF) ** 2
    basis = jnp.exp(-sharpness * (distance[:, None] - centers[None, :, None, None]) ** 2) * envelope[:, None]
    basis = basis.astype(jnp.bfloat16)
    partial_sums = jnp.einsum('prij,pjc->pric', basis.astype(jnp.float32), nbr_x.astype(jnp.float32), precision=lax.Precision.HIGHEST)
    return jnp.einsum('pric,rc->ic', partial_sums, rbf_mix, precision=lax.Precision.HIGHEST) * MSG_SCALE

def reference(embed, frac, pair_blocks, w_in, rbf_mix, w_charge, k_index, k_weight):
    feats = jnp.dot(embed.reshape(-1, HID), w_in, preferred_element_type=jnp.float32).astype(jnp.bfloat16).reshape(NBX, NBY, ATOMS_BLK, HID)
    frac_full = frac.astype(jnp.float32)

    def one_block(block_index):
        blk_row = block_index // NBY
        blk_col = block_index % NBY
        pair_codes = pair_blocks[blk_row, blk_col]
        step_x = pair_codes // 3 - 1
        step_y = pair_codes % 3 - 1
        near_row = (blk_row + step_x) % NBX
        near_col = (blk_col + step_y) % NBY
        return pair_messages(frac_full[blk_row, blk_col], frac_full[near_row, near_col], feats[near_row, near_col], step_x.astype(jnp.float32), step_y.astype(jnp.float32), rbf_mix)
    messages = lax.map(one_block, jnp.arange(NBX * NBY, dtype=jnp.int32)).reshape(NBX, NBY, ATOMS_BLK, HID)
    kvec_x = k_index[0].astype(jnp.float32) * (2.0 * math.pi / (NBX * CELL))
    kvec_y = k_index[1].astype(jnp.float32) * (2.0 * math.pi / (NBY * CELL))
    kvec_z = k_index[2].astype(jnp.float32) * (2.0 * math.pi / HEIGHT)

    def row_tables(blk_row):
        frac_row = frac_full[blk_row]
        block_x = blk_row.astype(jnp.float32)
        block_y = jnp.arange(NBY, dtype=jnp.int32).astype(jnp.float32)
        coords_x = ((block_x + frac_row[:, 0, :]) * CELL).reshape(-1)
        coords_y = ((block_y[:, None] + frac_row[:, 1, :]) * CELL).reshape(-1)
        coords_z = (frac_row[:, 2, :] * HEIGHT).reshape(-1)
        phases = coords_x[:, None] * kvec_x[None, :] + coords_y[:, None] * kvec_y[None, :] + coords_z[:, None] * kvec_z[None, :]
        charges = jnp.dot(embed[blk_row].reshape(-1, HID), w_charge, preferred_element_type=jnp.float32)
        return (jnp.cos(phases), jnp.sin(phases), charges)
    rows = jnp.arange(NBX, dtype=jnp.int32)

    def add_charge(carry, blk_row):
        cosines, sines, charges = row_tables(blk_row)
        return (carry + lax.optimization_barrier(jnp.sum(charges, axis=0)), None)
    charge_total, unused = lax.scan(add_charge, jnp.zeros((HID,), jnp.float32), rows)
    charge_mean = charge_total / ATOMS
    contract = (((0,), (0,)), ((), ()))

    def add_factors(carry, blk_row):
        cosines, sines, charges = row_tables(blk_row)
        centred = charges - charge_mean[None, :]
        part_cos = lax.dot_general(cosines, centred, contract, precision=lax.Precision.HIGHEST)
        part_sin = lax.dot_general(sines, centred, contract, precision=lax.Precision.HIGHEST)
        return ((carry[0] + part_cos, carry[1] + part_sin), None)
    start = (jnp.zeros((KVEC, HID), jnp.float32), jnp.zeros((KVEC, HID), jnp.float32))
    factors, unused = lax.scan(add_factors, start, rows)
    field_scale = 1.0 / math.sqrt(ATOMS * KVEC)
    weighted_cos = k_weight[:, None] * factors[0]
    weighted_sin = k_weight[:, None] * factors[1]

    def row_field(blk_row):
        cosines, sines, charges = row_tables(blk_row)
        field = jnp.dot(cosines, weighted_cos, precision=lax.Precision.HIGHEST) + jnp.dot(sines, weighted_sin, precision=lax.Precision.HIGHEST)
        return (field * field_scale).reshape(NBY, ATOMS_BLK, HID)
    field_all = lax.map(row_field, rows)
    return embed.astype(jnp.float32) + messages + field_all
```

```python
import functools
import math

import jax
import jax.numpy as jnp
from jax import lax
from jax.experimental import pallas as pl
from jax.experimental.pallas import tpu as pltpu
from jax.sharding import PartitionSpec as P

CELL = 5.0
HEIGHT = 51.2
MSG_SCALE = 0.5
LANES = 128
FRAC_ROWS = 16
TAIL = 32
MIB = 1024 * 1024

COS_POLY = (0.9999992251396179, -19.738981246948242, 64.92865753173828, -85.27162170410156, 58.79049301147461, -21.07110595703125)
SIN_POLY = (6.283185005187988, -41.341590881347656, 81.59994506835938, -76.61447143554688, 41.3428840637207, -12.471243858337402)
ENV_POLY = (0.9999998211860657, -0.23369461297988892, 0.019939105957746506, -0.000846334092784673)


def horner(coefs, s):
    acc = coefs[-1] * s + coefs[-2]
    for c in coefs[-3::-1]:
        acc = acc * s + c
    return acc


def outer_rows(d, nb):
    rhs = jnp.broadcast_to(d[nb : nb + 1], (8, LANES)) * 0.125
    return [
        lax.dot_general(
            jnp.broadcast_to(d[b : b + 1], (8, LANES)),
            rhs,
            (((0,), (0,)), ((), ())),
            precision=lax.Precision.HIGHEST,
            preferred_element_type=jnp.float32,
        )
        for b in range(nb)
    ]


def put_message(send_ref, half, state):
    hi = state.astype(jnp.bfloat16).astype(jnp.float32)
    rest = state - hi
    mid = rest.astype(jnp.bfloat16).astype(jnp.float32)
    low = rest - mid
    send_ref[half : half + TAIL, :] = jnp.concatenate([hi, mid, low, jnp.zeros_like(hi)], axis=0).astype(
        jnp.bfloat16
    )


def tables_kernel(nx, ny, frac_ref, kidx_ref, emb_ref, cs_ref, acc_ref, state_ref, send_ref, k16, x16, sums, states):
    rows, cols, _, atoms = frac_ref.shape
    kvec = kidx_ref.shape[1]
    nb = kvec // LANES
    n = rows * cols * atoms
    me_x, me_y = lax.axis_index("gx"), lax.axis_index("gy")
    kf = kidx_ref[...].astype(jnp.float32)
    k16[...] = jnp.zeros_like(k16)
    x16[...] = jnp.zeros_like(x16)
    k16[0:1, :] = kf[0:1] * (1.0 / nx)
    k16[1:2, :] = kf[0:1] * (1.0 / nx)
    k16[2:3, :] = kf[1:2] * (1.0 / ny)
    k16[3:4, :] = kf[1:2] * (1.0 / ny)
    k16[4:5, :] = kf[2:3]
    for r in range(rows):
        for c in range(cols):
            at = slice((r * cols + c) * atoms, (r * cols + c + 1) * atoms)
            f = frac_ref[r, c].astype(jnp.float32)
            x16[0:1, at] = jnp.full((1, atoms), me_x * rows + r, jnp.int32).astype(jnp.float32)
            x16[1:2, at] = f[0:1]
            x16[2:3, at] = jnp.full((1, atoms), me_y * cols + c, jnp.int32).astype(jnp.float32)
            x16[3:4, at] = f[1:2]
            x16[4:5, at] = f[2:3]
    kb = k16[...].astype(jnp.bfloat16)
    xb = x16[...].astype(jnp.bfloat16)
    for b in range(nb):
        turns = lax.dot_general(
            kb[:, b * LANES : (b + 1) * LANES], xb, (((0,), (0,)), ((), ())), preferred_element_type=jnp.float32
        )
        turns = turns - jnp.round(turns)
        square = turns * turns
        cs_ref[b * LANES : (b + 1) * LANES, :] = horner(COS_POLY, square).astype(jnp.bfloat16)
        cs_ref[kvec + b * LANES : kvec + (b + 1) * LANES, :] = (turns * horner(SIN_POLY, square)).astype(
            jnp.bfloat16
        )
    emb = emb_ref[...]
    ones = jnp.ones((16, n), jnp.bfloat16)
    mean = jnp.dot(ones, emb, preferred_element_type=jnp.float32)[0:1] * (1.0 / n)
    states[...] = jnp.zeros_like(states)
    for h in range(2):
        table = cs_ref[h * kvec : (h + 1) * kvec, :]
        count = lax.dot_general(ones, table, (((1,), (1,)), ((), ())), preferred_element_type=jnp.float32)
        for b in range(nb):
            states[h, b : b + 1, :] = count[0:1, b * LANES : (b + 1) * LANES]
        states[h, nb : nb + 1, :] = mean
        total = jnp.dot(table, emb, preferred_element_type=jnp.float32)
        for b, part in enumerate(outer_rows(states[h], nb)):
            sums[h, b * LANES : (b + 1) * LANES, :] = total[b * LANES : (b + 1) * LANES] - part
    core = lax.rem(me_x, 2)
    acc_ref[...] = sums[core]
    state_ref[...] = states[core]
    send_ref[0:kvec, :] = sums[1 - core].astype(jnp.bfloat16)
    put_message(send_ref, kvec, states[1 - core])


def merge_kernel(last, acc_ref, state_ref, got_ref, *outs):
    half = acc_ref.shape[0]
    nb = half // LANES
    tail = got_ref[half : half + TAIL, :].astype(jnp.float32)
    theirs = tail[0:8] + tail[8:16] + tail[16:24]
    mine = state_ref[...]
    row = lax.broadcasted_iota(jnp.int32, (8, LANES), 0)
    state = (mine + theirs) * jnp.where(row < nb, 1.0, 0.5)
    diff = (mine - theirs) * jnp.where(row < nb, 1.0, 0.5)
    for b, part in enumerate(outer_rows(diff, nb)):
        at = slice(b * LANES, (b + 1) * LANES)
        merged = acc_ref[at, :] + got_ref[at, :].astype(jnp.float32) + part
        if not last:
            outs[1][at, :] = merged
        outs[0][at, :] = merged.astype(jnp.bfloat16)
    if not last:
        outs[2][...] = state
        put_message(outs[0], half, state)


def pair_kernel(codes_ref, ext_ref, got1_ref, got2_ref, w_ref, mix_ref, out_ref, fields, feats, basis, gathered):
    rows, width, packed, channels = ext_ref.shape
    atoms = packed - FRAC_ROWS
    cols = width - 2
    npb = codes_ref.shape[-1]
    nrbf = mix_ref.shape[0]
    core = lax.rem(lax.axis_index("gx"), 2)
    w = w_ref[...]

    def take(slot, block):
        feats[slot] = jnp.dot(block[:atoms], w, preferred_element_type=jnp.float32).astype(jnp.bfloat16)
        fields[slot] = block[atoms:].astype(jnp.float32)[0:8]

    for r in range(rows):
        for c in range(width):
            take((r + 1) * width + c, ext_ref[r, c])

    def halo(before_ref, after_ref):
        for c in range(width):
            take(c, before_ref[c])
            take((rows + 1) * width + c, after_ref[c])

    @pl.when(core == 0)
    def _():
        halo(got2_ref, got1_ref)

    @pl.when(core == 1)
    def _():
        halo(got1_ref, got2_ref)

    order = lax.broadcasted_iota(jnp.int32, (nrbf, channels), 0).astype(jnp.float32) - nrbf // 2
    mix = mix_ref[...] * (jnp.exp(-order * order) * MSG_SCALE)

    def column(index, carry):
        r, c = index // cols, index % cols
        own = fields[(r + 1) * width + c + 1]
        own = jnp.transpose(jnp.concatenate([own] * (LANES // 8), axis=0))
        own_x = jnp.broadcast_to(own[:, 0:1] * CELL, (atoms, atoms))
        own_y = jnp.broadcast_to(own[:, 1:2] * CELL, (atoms, atoms))
        own_z = jnp.broadcast_to(own[:, 2:3] * HEIGHT, (atoms, atoms))
        for p in range(npb):
            code = codes_ref[index, p]
            step_x, step_y = code // 3 - 1, code % 3 - 1
            slot = (r + 1 + step_x) * width + c + 1 + step_y
            near = fields[slot]
            dx = (near[0:1] + step_x.astype(jnp.float32)) * CELL - own_x
            dy = (near[1:2] + step_y.astype(jnp.float32)) * CELL - own_y
            dz = jnp.abs(near[2:3] * HEIGHT - own_z)
            dz = jnp.minimum(dz, HEIGHT - dz)
            s = jnp.minimum((dx * dx + dy * dy + dz * dz) * (1.0 / (CELL * CELL)), 1.0)
            root = s * lax.rsqrt(jnp.maximum(s, 1e-30))
            z = root * (nrbf - 1.0) - nrbf // 2
            env = (1.0 - s) * horner(ENV_POLY, s)
            mid = env * env * jnp.exp(-z * z)
            up, down = jnp.exp(2.0 * z), jnp.exp(-2.0 * z)
            at = slice(p * atoms, (p + 1) * atoms)
            value = mid
            for q in range(nrbf // 2, nrbf):
                basis[q * atoms : (q + 1) * atoms, at] = value.astype(jnp.bfloat16)
                value = value * up
            value = mid
            for q in range(nrbf // 2 - 1, -1, -1):
                value = value * down
                basis[q * atoms : (q + 1) * atoms, at] = value.astype(jnp.bfloat16)
            gathered[at, :] = feats[slot]
        parts = jnp.dot(basis[...], gathered[...], preferred_element_type=jnp.float32)
        total = parts[0:atoms] * mix[0:1]
        for q in range(1, nrbf):
            total = total + parts[q * atoms : (q + 1) * atoms] * mix[q : q + 1]
        out_ref[index] = total
        return carry

    lax.fori_loop(0, rows * cols, column, 0)


def field_kernel(scale, mine_ref, theirs_ref, weight_ref, w_ref, cs_ref, emb_ref, msg_ref, out_ref):
    kvec = mine_ref.shape[0]
    cells, atoms, _ = out_ref.shape
    first = lax.rem(lax.axis_index("gx"), 2) == 0
    mine, theirs = mine_ref[...].astype(jnp.float32), theirs_ref[...].astype(jnp.float32)
    w_t = jnp.transpose(w_ref[...].astype(jnp.float32)).astype(jnp.bfloat16)
    weight = weight_ref[...] * scale
    total = None
    for h in range(2):
        half = jnp.where(first, mine, theirs) if h == 0 else jnp.where(first, theirs, mine)
        factors = lax.dot_general(
            w_t, half.astype(jnp.bfloat16), (((1,), (1,)), ((), ())), preferred_element_type=jnp.float32
        )
        part = jnp.dot(
            (factors * weight).astype(jnp.bfloat16),
            cs_ref[h * kvec : (h + 1) * kvec, :],
            preferred_element_type=jnp.float32,
        )
        total = part if total is None else total + part
    for i in range(cells):
        out_ref[i] = (
            emb_ref[i * atoms : (i + 1) * atoms, :].astype(jnp.float32)
            + msg_ref[i]
            + jnp.transpose(total[:, i * atoms : (i + 1) * atoms])
        )


def vmem(count):
    return [pl.BlockSpec(memory_space=pltpu.VMEM)] * count


def shards(embed, frac, pair_blocks, w_in, rbf_mix, w_charge, k_index, k_weight):
    f32, bf16 = jnp.float32, jnp.bfloat16
    rows, cols, atoms, channels = embed.shape
    kvec = k_weight.shape[0]
    size_x, size_y = lax.axis_size("gx"), lax.axis_size("gy")
    count = size_x * size_y
    both = ("gx", "gy")
    cells = rows * cols
    atoms_all = cells * count * atoms
    flat = embed.reshape(-1, channels)
    params = functools.partial(pltpu.CompilerParams, vmem_limit_bytes=32 * MIB)

    packed = jnp.concatenate([embed, jnp.pad(frac, ((0, 0), (0, 0), (0, FRAC_ROWS - frac.shape[2]), (0, 0)))], axis=2)
    if size_y == 2:
        got = lax.ppermute(jnp.stack([packed[:, -1], packed[:, 0]], axis=1), "gy", [(0, 1), (1, 0)])
        west, east = got[:, 0:1], got[:, 1:2]
    else:
        west = lax.ppermute(packed[:, -1:], "gy", [(i, (i + 1) % size_y) for i in range(size_y)])
        east = lax.ppermute(packed[:, :1], "gy", [((i + 1) % size_y, i) for i in range(size_y)])
    ext = jnp.concatenate([west, packed, east], axis=1)
    core = lax.rem(lax.axis_index("gx"), 2)
    toward_1 = lax.dynamic_index_in_dim(ext, jnp.where(core == 0, rows - 1, 0), 0, keepdims=False)
    toward_2 = lax.dynamic_index_in_dim(ext, jnp.where(core == 0, 0, rows - 1), 0, keepdims=False)
    got_1 = lax.ppermute(toward_1, "gx", [(i, i ^ 1) for i in range(size_x)])
    got_2 = lax.ppermute(
        toward_2, "gx", [(i, (i - 1) % size_x if i % 2 == 0 else (i + 1) % size_x) for i in range(size_x)]
    )

    table, acc, state, send = pl.pallas_call(
        functools.partial(tables_kernel, rows * size_x, cols * size_y),
        out_shape=[
            jax.ShapeDtypeStruct((2 * kvec, cells * atoms), bf16),
            jax.ShapeDtypeStruct((kvec, channels), f32),
            jax.ShapeDtypeStruct((8, LANES), f32),
            jax.ShapeDtypeStruct((kvec + TAIL, channels), bf16),
        ],
        in_specs=vmem(3),
        out_specs=vmem(4),
        scratch_shapes=[
            pltpu.VMEM((16, kvec), f32),
            pltpu.VMEM((16, cells * atoms), f32),
            pltpu.VMEM((2, kvec, channels), f32),
            pltpu.VMEM((2, 8, LANES), f32),
        ],
        compiler_params=params(),
        name="tables",
    )(frac, k_index, flat)

    def merge(acc, state, got, last):
        out_shape = [jax.ShapeDtypeStruct((kvec if last else kvec + TAIL, channels), bf16)]
        if not last:
            out_shape += [jax.ShapeDtypeStruct(acc.shape, f32), jax.ShapeDtypeStruct(state.shape, f32)]
        return pl.pallas_call(
            functools.partial(merge_kernel, last),
            out_shape=out_shape,
            in_specs=vmem(3),
            out_specs=vmem(len(out_shape)),
            compiler_params=params(),
            name="merge",
        )(acc, state, got)

    def exchange(values, mask_of):
        return lax.ppermute(values, both, [(i, i ^ mask_of(i)) for i in range(count)])

    core_bit = size_y
    masks = [1 << b for b in range(count.bit_length() - 1) if 1 << b != core_bit]
    swapped = [masks[t ^ 1] if t ^ 1 < len(masks) else masks[t] for t in range(len(masks))]
    send, acc, state = merge(acc, state, exchange(send, lambda i: core_bit), False)
    for t in range(len(masks)):
        last = t == len(masks) - 1
        got = exchange(send, lambda i, t=t: swapped[t] if i & core_bit else masks[t])
        if last:
            (mine,) = merge(acc, state, got, True)
        else:
            send, acc, state = merge(acc, state, got, False)
    theirs = exchange(mine, lambda i: core_bit)

    width = cols + 2
    npb = pair_blocks.shape[-1]
    nrbf = rbf_mix.shape[0]
    slots = (rows + 2) * width
    messages = pl.pallas_call(
        pair_kernel,
        out_shape=jax.ShapeDtypeStruct((cells, atoms, channels), f32),
        in_specs=[pl.BlockSpec(memory_space=pltpu.SMEM)] + vmem(5),
        out_specs=pl.BlockSpec(memory_space=pltpu.VMEM),
        scratch_shapes=[
            pltpu.VMEM((slots, 8, atoms), f32),
            pltpu.VMEM((slots, atoms, channels), bf16),
            pltpu.VMEM((nrbf * atoms, npb * atoms), bf16),
            pltpu.VMEM((npb * atoms, channels), bf16),
        ],
        compiler_params=params(),
        name="pairs",
    )(pair_blocks.reshape(cells, npb), ext, got_1, got_2, w_in, rbf_mix)

    updated = pl.pallas_call(
        functools.partial(field_kernel, 1.0 / math.sqrt(atoms_all * kvec)),
        out_shape=jax.ShapeDtypeStruct((cells, atoms, channels), f32),
        in_specs=vmem(7),
        out_specs=pl.BlockSpec(memory_space=pltpu.VMEM),
        compiler_params=params(),
        name="field",
    )(mine, theirs, k_weight.reshape(1, kvec), w_charge, table, flat, messages)
    return updated.reshape(embed.shape)


def solution(mesh):
    in_specs = (
        P("gx", "gy", None, None),
        P("gx", "gy", None, None),
        P("gx", "gy", None),
        P(),
        P(),
        P(),
        P(),
        P(),
    )
    out_specs = P("gx", "gy", None, None)
    return jax.shard_map(shards, mesh=mesh, in_specs=in_specs, out_specs=out_specs, check_vma=False)
```

```python
import functools
import math

import jax
import jax.numpy as jnp
from jax import lax
from jax.experimental import pallas as pl
from jax.experimental.pallas import tpu as pltpu
from jax.sharding import PartitionSpec as P

CELL = 5.0
HEIGHT = 51.2
MSG_SCALE = 0.5
LANES = 128
FRAC_ROWS = 16
TAIL = 32
MIB = 1024 * 1024

COS_POLY = (0.9999992251396179, -19.738981246948242, 64.92865753173828, -85.27162170410156, 58.79049301147461, -21.07110595703125)
SIN_POLY = (6.283185005187988, -41.341590881347656, 81.59994506835938, -76.61447143554688, 41.3428840637207, -12.471243858337402)
ENV_POLY = (0.9999998211860657, -0.23369461297988892, 0.019939105957746506, -0.000846334092784673)


def horner(coefs, s):
    acc = coefs[-1] * s + coefs[-2]
    for c in coefs[-3::-1]:
        acc = acc * s + c
    return acc


def outer_row(column, row):
    return lax.dot_general(
        jnp.broadcast_to(column, (8, LANES)),
        jnp.broadcast_to(row, (8, LANES)) * 0.125,
        (((0,), (0,)), ((), ())),
        precision=lax.Precision.HIGHEST,
        preferred_element_type=jnp.float32,
    )


def put_message(send_ref, half, state):
    hi = state.astype(jnp.bfloat16).astype(jnp.float32)
    rest = state - hi
    mid = rest.astype(jnp.bfloat16).astype(jnp.float32)
    low = rest - mid
    send_ref[half : half + TAIL, :] = jnp.concatenate([hi, mid, low, jnp.zeros_like(hi)], axis=0).astype(
        jnp.bfloat16
    )


def tables_kernel(sent, nx, ny, frac_ref, kidx_ref, emb_ref, after_ref, *refs):
    del after_ref
    if sent:
        table_ref, send_ref, k16, x16, state_ref = refs
    else:
        table_ref, acc_ref, state_ref, k16, x16 = refs
    rows, cols, _, atoms = frac_ref.shape
    kvec = kidx_ref.shape[1]
    nb = kvec // LANES
    n = rows * cols * atoms
    me_x, me_y = lax.axis_index("gx"), lax.axis_index("gy")
    core = lax.rem(me_x, 2)
    half = 1 - core if sent else core
    offset = half.astype(jnp.float32) * 0.25
    kf = kidx_ref[...].astype(jnp.float32)
    k16[...] = jnp.zeros_like(k16)
    x16[...] = jnp.zeros_like(x16)
    k16[0:1, :] = kf[0:1] * (1.0 / nx)
    k16[1:2, :] = kf[0:1] * (1.0 / nx)
    k16[2:3, :] = kf[1:2] * (1.0 / ny)
    k16[3:4, :] = kf[1:2] * (1.0 / ny)
    k16[4:5, :] = kf[2:3]
    for r in range(rows):
        for c in range(cols):
            at = slice((r * cols + c) * atoms, (r * cols + c + 1) * atoms)
            f = frac_ref[r, c].astype(jnp.float32)
            x16[0:1, at] = jnp.full((1, atoms), me_x * rows + r, jnp.int32).astype(jnp.float32)
            x16[1:2, at] = f[0:1]
            x16[2:3, at] = jnp.full((1, atoms), me_y * cols + c, jnp.int32).astype(jnp.float32)
            x16[3:4, at] = f[1:2]
            x16[4:5, at] = f[2:3]
    kb = k16[...].astype(jnp.bfloat16)
    xb = x16[...].astype(jnp.bfloat16)
    emb = emb_ref[...]
    ones = jnp.ones((16, n), jnp.bfloat16)
    mean = jnp.dot(ones, emb, preferred_element_type=jnp.float32)[0:1] * (1.0 / n)
    state_ref[...] = jnp.zeros_like(state_ref)
    state_ref[nb : nb + 1, :] = mean
    for b in range(nb):
        at = slice(b * LANES, (b + 1) * LANES)
        turns = lax.dot_general(kb[:, at], xb, (((0,), (0,)), ((), ())), preferred_element_type=jnp.float32)
        turns = turns - offset
        turns = turns - jnp.round(turns)
        table = horner(COS_POLY, turns * turns).astype(jnp.bfloat16)
        table_ref[at, :] = table
        count = lax.dot_general(ones, table, (((1,), (1,)), ((), ())), preferred_element_type=jnp.float32)
        state_ref[b : b + 1, :] = count[0:1]
        centred = jnp.dot(table, emb, preferred_element_type=jnp.float32) - outer_row(count[0:1], mean)
        if sent:
            send_ref[at, :] = centred.astype(jnp.bfloat16)
        else:
            acc_ref[at, :] = centred
    if sent:
        put_message(send_ref, kvec, state_ref[...])


def merge_kernel(last, acc_ref, state_ref, got_ref, after_ref, *outs):
    del after_ref
    half = acc_ref.shape[0]
    nb = half // LANES
    tail = got_ref[half : half + TAIL, :].astype(jnp.float32)
    theirs = tail[0:8] + tail[8:16] + tail[16:24]
    mine = state_ref[...]
    weight = jnp.where(lax.broadcasted_iota(jnp.int32, (8, LANES), 0) < nb, 1.0, 0.5)
    state = (mine + theirs) * weight
    diff = (mine - theirs) * weight
    for b in range(nb):
        at = slice(b * LANES, (b + 1) * LANES)
        part = outer_row(diff[b : b + 1], diff[nb : nb + 1])
        merged = acc_ref[at, :] + got_ref[at, :].astype(jnp.float32) + part
        if not last:
            outs[1][at, :] = merged
        outs[0][at, :] = merged.astype(jnp.bfloat16)
    if not last:
        outs[2][...] = state
        put_message(outs[0], half, state)


def feats_kernel(frac_ref, emb_ref, w_ref, after_ref, out_ref):
    del after_ref
    rows, cols, parts, atoms = frac_ref.shape
    feats = jnp.dot(emb_ref[...], w_ref[...], preferred_element_type=jnp.float32).astype(jnp.bfloat16)
    for r in range(rows):
        for c in range(cols):
            at = (r * cols + c) * atoms
            out_ref[r, c, 0:atoms, :] = feats[at : at + atoms]
            f = frac_ref[r, c].astype(jnp.float32)
            f = jnp.concatenate([f, jnp.zeros((FRAC_ROWS - parts, atoms), jnp.float32)], axis=0)
            out_ref[r, c, atoms : atoms + FRAC_ROWS, :] = f.astype(jnp.bfloat16)


def pair_kernel(first, codes_ref, ext_ref, got_ref, mix_ref, after_ref, out_ref, near3, fields, basis, gathered):
    del after_ref
    rows, width, packed, channels = ext_ref.shape
    atoms = packed - FRAC_ROWS
    cols = width - 2
    npb = codes_ref.shape[-1]
    nrbf = mix_ref.shape[0]
    core = lax.rem(lax.axis_index("gx"), 2)
    above = core if first else 1 - core
    row = 1 - above

    @pl.when(above == 0)
    def _():
        near3[0:rows] = ext_ref[...]
        near3[rows] = got_ref[...]

    @pl.when(above == 1)
    def _():
        near3[0] = got_ref[...]
        near3[1 : rows + 1] = ext_ref[...]

    for r in range(rows + 1):
        for c in range(width):
            fields[r * width + c] = near3[r, c, atoms:packed, :].astype(jnp.float32)[0:8]

    order = lax.broadcasted_iota(jnp.int32, (nrbf, channels), 0).astype(jnp.float32) - nrbf // 2
    mix = mix_ref[...] * (jnp.exp(-order * order) * MSG_SCALE)
    bits = math.sqrt(math.log2(math.e))

    for c in range(cols):
        own = fields[width + c + 1]
        own = jnp.transpose(jnp.concatenate([own] * (LANES // 8), axis=0))
        own_x = jnp.broadcast_to(own[:, 0:1], (atoms, atoms))
        own_y = jnp.broadcast_to(own[:, 1:2], (atoms, atoms))
        own_z = jnp.broadcast_to(own[:, 2:3] * (HEIGHT / CELL), (atoms, atoms))
        slot = c % 2
        for p in range(npb):
            code = codes_ref[row, c, p]
            step_x, step_y = code // 3 - 1, code % 3 - 1
            near = fields[(1 + step_x) * width + c + 1 + step_y]
            dx = (near[0:1] + step_x.astype(jnp.float32)) - own_x
            dy = (near[1:2] + step_y.astype(jnp.float32)) - own_y
            dz = jnp.abs(near[2:3] * (HEIGHT / CELL) - own_z)
            dz = jnp.minimum(dz, HEIGHT / CELL - dz)
            s = jnp.minimum(dx * dx + dy * dy + dz * dz, 1.0)
            root = s * lax.rsqrt(jnp.maximum(s, 1e-30))
            z = root * (bits * (nrbf - 1)) - bits * (nrbf // 2)
            env = (1.0 - s) * horner(ENV_POLY, s)
            mid = env * env * jnp.exp2(-(z * z))
            up, down = jnp.exp2((2.0 * bits) * z), jnp.exp2((-2.0 * bits) * z)
            at = slice(p * atoms, (p + 1) * atoms)
            value = mid
            for q in range(nrbf // 2, nrbf):
                basis[slot, q * atoms : (q + 1) * atoms, at] = value.astype(jnp.bfloat16)
                value = value * up
            value = mid
            for q in range(nrbf // 2 - 1, -1, -1):
                value = value * down
                basis[slot, q * atoms : (q + 1) * atoms, at] = value.astype(jnp.bfloat16)
            gathered[slot, at, :] = near3[1 + step_x, c + 1 + step_y, 0:atoms, :]
        parts = jnp.dot(basis[slot], gathered[slot], preferred_element_type=jnp.float32)
        total = parts[0:atoms] * mix[0:1]
        for q in range(1, nrbf):
            total = total + parts[q * atoms : (q + 1) * atoms] * mix[q : q + 1]
        out_ref[c] = total


def field_part(scale, half_ref, weight_ref, w_ref, table_ref):
    w_t = jnp.transpose(w_ref[...].astype(jnp.float32)).astype(jnp.bfloat16)
    factors = lax.dot_general(w_t, half_ref[...], (((1,), (1,)), ((), ())), preferred_element_type=jnp.float32)
    factors = (factors * (weight_ref[...] * scale)).astype(jnp.bfloat16)
    return jnp.dot(factors, table_ref[...], preferred_element_type=jnp.float32)


def own_field_kernel(scale, half_ref, weight_ref, w_ref, table_ref, emb_ref, msg1_ref, msg2_ref, out_ref):
    cols, atoms, _ = msg1_ref.shape
    row1 = 1 - lax.rem(lax.axis_index("gx"), 2)
    total = field_part(scale, half_ref, weight_ref, w_ref, table_ref)
    for r in range(2):
        for c in range(cols):
            i = r * cols + c
            at = slice(i * atoms, (i + 1) * atoms)
            msg = jnp.where(row1 == r, msg1_ref[c], msg2_ref[c])
            out_ref[i] = emb_ref[at, :].astype(jnp.float32) + msg + jnp.transpose(total[:, at])


def other_field_kernel(scale, half_ref, weight_ref, w_ref, table_ref, part_ref, out_ref):
    cells, atoms, _ = out_ref.shape
    total = field_part(scale, half_ref, weight_ref, w_ref, table_ref)
    for i in range(cells):
        out_ref[i] = part_ref[i] + jnp.transpose(total[:, i * atoms : (i + 1) * atoms])


def vmem(count):
    return [pl.BlockSpec(memory_space=pltpu.VMEM)] * count


def shards(embed, frac, pair_blocks, w_in, rbf_mix, w_charge, k_index, k_weight):
    f32, bf16 = jnp.float32, jnp.bfloat16
    rows, cols, atoms, channels = embed.shape
    kvec = k_weight.shape[0]
    npb = pair_blocks.shape[-1]
    nrbf = rbf_mix.shape[0]
    size_x, size_y = lax.axis_size("gx"), lax.axis_size("gy")
    count = size_x * size_y
    cells = rows * cols
    width = cols + 2
    flat = embed.reshape(-1, channels)
    unread = [pl.BlockSpec(memory_space=pl.ANY)]

    def call(body, name, ins, outs, scratch=(), smem=0, after=None):
        specs = [pl.BlockSpec(memory_space=pltpu.SMEM)] * smem + vmem(len(ins) - smem)
        if after is not None:
            ins, specs = [*ins, after], specs + unread
        return pl.pallas_call(
            body,
            out_shape=[jax.ShapeDtypeStruct(*o) for o in outs],
            in_specs=specs,
            out_specs=vmem(len(outs)),
            scratch_shapes=[pltpu.VMEM(*s) for s in scratch],
            compiler_params=pltpu.CompilerParams(vmem_limit_bytes=32 * MIB),
            name=name,
        )(*ins)

    def exchange(values, mask_of):
        return lax.ppermute(values, ("gx", "gy"), [(i, i ^ mask_of(i)) for i in range(count)])

    acc_out, state_out = ((kvec, channels), f32), ((8, LANES), f32)
    send_out = ((kvec + TAIL, channels), bf16)
    table_out = ((kvec, cells * atoms), bf16)
    k16, x16 = ((16, kvec), f32), ((16, cells * atoms), f32)
    shape = (rows * size_x, cols * size_y)
    table_theirs, send = call(
        functools.partial(tables_kernel, True, *shape), "sent_half",
        [frac, k_index, flat], [table_out, send_out], [k16, x16, state_out], after=k_weight,
    )
    table_mine, acc, state = call(
        functools.partial(tables_kernel, False, *shape), "kept_half",
        [frac, k_index, flat], [table_out, acc_out, state_out], [k16, x16], after=table_theirs,
    )

    def merge(acc, state, got, after, last=False):
        outs = [((kvec, channels), bf16)] if last else [send_out, acc_out, state_out]
        return call(functools.partial(merge_kernel, last), "merge", [acc, state, got], outs, after=after)

    core_bit = size_y
    masks = [1 << b for b in range(count.bit_length() - 1) if 1 << b != core_bit]
    swapped = [masks[t ^ 1] if t ^ 1 < len(masks) else masks[t] for t in range(len(masks))]

    def cross(send, t):
        return exchange(send, lambda i: swapped[t] if i & core_bit else masks[t])

    send, acc, state = merge(acc, state, exchange(send, lambda i: core_bit), table_mine)

    got = cross(send, 0)
    (packed,) = call(
        feats_kernel, "feats", [frac, flat, w_in], [((rows, cols, atoms + FRAC_ROWS, channels), bf16)], after=state
    )
    if size_y == 2:
        edges = lax.ppermute(jnp.stack([packed[:, -1], packed[:, 0]], axis=1), "gy", [(0, 1), (1, 0)])
        west, east = edges[:, 0:1], edges[:, 1:2]
    else:
        west = lax.ppermute(packed[:, -1:], "gy", [(i, (i + 1) % size_y) for i in range(size_y)])
        east = lax.ppermute(packed[:, :1], "gy", [((i + 1) % size_y, i) for i in range(size_y)])
    send, acc, state = merge(acc, state, got, packed)

    got = cross(send, 1)
    ext = jnp.concatenate([west, packed, east], axis=1)
    core = lax.rem(lax.axis_index("gx"), 2)
    toward_1 = lax.dynamic_index_in_dim(ext, 1 - core, 0, keepdims=False)
    toward_2 = lax.dynamic_index_in_dim(ext, core, 0, keepdims=False)
    got_1 = lax.ppermute(toward_1, "gx", [(i, i ^ 1) for i in range(size_x)])
    got_2 = lax.ppermute(
        toward_2, "gx", [(i, (i - 1) % size_x if i % 2 == 0 else (i + 1) % size_x) for i in range(size_x)]
    )
    send, acc, state = merge(acc, state, got, ext)

    def pairs(first, got_row, after):
        (out,) = call(
            functools.partial(pair_kernel, first), "pairs",
            [pair_blocks, ext, got_row, rbf_mix], [((cols, atoms, channels), f32)],
            [
                ((rows + 1, width, atoms + FRAC_ROWS, channels), bf16),
                (((rows + 1) * width, 8, atoms), f32),
                ((2, nrbf * atoms, npb * atoms), bf16),
                ((2, npb * atoms, channels), bf16),
            ],
            smem=1, after=after,
        )
        return out

    messages = [None, None]
    for t in range(2, len(masks)):
        got = cross(send, t)
        after = state
        if t < 4:
            after = messages[t - 2] = pairs(t == 2, got_1 if t == 2 else got_2, state)
        if t < len(masks) - 1:
            send, acc, state = merge(acc, state, got, after)
    (mine,) = merge(acc, state, got, after, last=True)
    theirs = exchange(mine, lambda i: core_bit)

    scale = 1.0 / math.sqrt(cells * count * atoms * kvec)
    weight = k_weight.reshape(1, kvec)
    out = ((cells, atoms, channels), f32)
    (part,) = call(
        functools.partial(own_field_kernel, scale), "own_field",
        [mine, weight, w_charge, table_mine, flat, *messages], [out],
    )
    (updated,) = call(
        functools.partial(other_field_kernel, scale), "other_field",
        [theirs, weight, w_charge, table_theirs, part], [out],
    )
    return updated.reshape(embed.shape)


def solution(mesh):
    in_specs = (
        P("gx", "gy", None, None),
        P("gx", "gy", None, None),
        P("gx", "gy", None),
        P(),
        P(),
        P(),
        P(),
        P(),
    )
    out_specs = P("gx", "gy", None, None)
    return jax.shard_map(shards, mesh=mesh, in_specs=in_specs, out_specs=out_specs, check_vma=False)
```

```python
import functools
import math

import jax
import jax.numpy as jnp
from jax import lax
from jax.experimental import pallas as pl
from jax.experimental.pallas import tpu as pltpu
from jax.sharding import PartitionSpec as P

CELL = 5.0
HEIGHT = 51.2
MSG_SCALE = 0.5
LANES = 128
FRAC_ROWS = 16
TAIL = 32
MIB = 1024 * 1024

COS_POLY = (0.9999992251396179, -19.738981246948242, 64.92865753173828, -85.27162170410156, 58.79049301147461, -21.07110595703125)
SIN_POLY = (6.283185005187988, -41.341590881347656, 81.59994506835938, -76.61447143554688, 41.3428840637207, -12.471243858337402)
ENV_POLY = (0.9999998211860657, -0.23369461297988892, 0.019939105957746506, -0.000846334092784673)


def horner(coefs, s):
    acc = coefs[-1] * s + coefs[-2]
    for c in coefs[-3::-1]:
        acc = acc * s + c
    return acc


def pieces(x):
    hi = x.astype(jnp.bfloat16).astype(jnp.float32)
    rest = x - hi
    mid = rest.astype(jnp.bfloat16).astype(jnp.float32)
    return hi, mid, rest - mid


def stack(rows, order):
    row = lax.broadcasted_iota(jnp.int32, (16, LANES), 0)
    out = jnp.zeros((16, LANES), jnp.float32)
    for at, which in enumerate(order):
        out = jnp.where(row == at, jnp.broadcast_to(rows[which], (16, LANES)), out)
    return out.astype(jnp.bfloat16)


def outer_row(column, row):
    return lax.dot_general(
        stack(column, (0, 0, 0, 1, 1, 2)), row, (((0,), (0,)), ((), ())), preferred_element_type=jnp.float32
    )


def row_stack(row):
    return stack(pieces(row), (0, 1, 2, 0, 1, 0))


def put_message(send_ref, half, state):
    parts = [*pieces(state), jnp.zeros_like(state)]
    send_ref[half : half + TAIL, :] = jnp.concatenate(parts, axis=0).astype(jnp.bfloat16)


def tables_kernel(sent, nx, ny, frac_ref, kidx_ref, emb_ref, after_ref, *refs):
    del after_ref
    if sent:
        table_ref, send_ref, k16, x16, state_ref = refs
    else:
        table_ref, acc_ref, state_ref, k16, x16 = refs
    rows, cols, _, atoms = frac_ref.shape
    kvec = kidx_ref.shape[1]
    nb = kvec // LANES
    n = rows * cols * atoms
    me_x, me_y = lax.axis_index("gx"), lax.axis_index("gy")
    core = lax.rem(me_x, 2)
    half = 1 - core if sent else core
    offset = half.astype(jnp.float32) * 0.25
    kf = kidx_ref[...].astype(jnp.float32)
    k16[...] = jnp.zeros_like(k16)
    x16[...] = jnp.zeros_like(x16)
    k16[0:1, :] = kf[0:1] * (1.0 / nx)
    k16[1:2, :] = kf[0:1] * (1.0 / nx)
    k16[2:3, :] = kf[1:2] * (1.0 / ny)
    k16[3:4, :] = kf[1:2] * (1.0 / ny)
    k16[4:5, :] = kf[2:3]
    for r in range(rows):
        for c in range(cols):
            at = slice((r * cols + c) * atoms, (r * cols + c + 1) * atoms)
            f = frac_ref[r, c].astype(jnp.float32)
            x16[0:1, at] = jnp.full((1, atoms), me_x * rows + r, jnp.int32).astype(jnp.float32)
            x16[1:2, at] = f[0:1]
            x16[2:3, at] = jnp.full((1, atoms), me_y * cols + c, jnp.int32).astype(jnp.float32)
            x16[3:4, at] = f[1:2]
            x16[4:5, at] = f[2:3]
    kb = k16[...].astype(jnp.bfloat16)
    xb = x16[...].astype(jnp.bfloat16)
    emb = emb_ref[...]
    ones = jnp.ones((16, n), jnp.bfloat16)
    mean = jnp.dot(ones, emb, preferred_element_type=jnp.float32)[0:1] * (1.0 / n)
    state_ref[...] = jnp.zeros_like(state_ref)
    state_ref[nb : nb + 1, :] = mean
    mean = row_stack(mean)
    for b in range(nb):
        at = slice(b * LANES, (b + 1) * LANES)
        turns = lax.dot_general(kb[:, at], xb, (((0,), (0,)), ((), ())), preferred_element_type=jnp.float32)
        turns = turns - offset
        turns = turns - jnp.round(turns)
        table = horner(COS_POLY, turns * turns).astype(jnp.bfloat16)
        table_ref[at, :] = table
        count = lax.dot_general(ones, table, (((1,), (1,)), ((), ())), preferred_element_type=jnp.float32)
        state_ref[b : b + 1, :] = count[0:1]
        centred = jnp.dot(table, emb, preferred_element_type=jnp.float32) - outer_row(pieces(count[0:1]), mean)
        if sent:
            send_ref[at, :] = centred.astype(jnp.bfloat16)
        else:
            acc_ref[at, :] = centred
    if sent:
        put_message(send_ref, kvec, state_ref[...])


def merge_kernel(last, acc_ref, state_ref, got_ref, after_ref, *outs):
    del after_ref
    half = acc_ref.shape[0]
    nb = half // LANES
    tail = got_ref[half : half + TAIL, :].astype(jnp.float32)
    theirs = tail[0:8] + tail[8:16] + tail[16:24]
    mine = state_ref[...]
    weight = jnp.where(lax.broadcasted_iota(jnp.int32, (8, LANES), 0) < nb, 1.0, 0.5)
    state = (mine + theirs) * weight
    diff = (mine - theirs) * weight
    split = pieces(diff)
    means = row_stack(diff[nb : nb + 1])
    for b in range(nb):
        at = slice(b * LANES, (b + 1) * LANES)
        part = outer_row([piece[b : b + 1] for piece in split], means)
        merged = acc_ref[at, :] + got_ref[at, :].astype(jnp.float32) + part
        if not last:
            outs[1][at, :] = merged
        outs[0][at, :] = merged.astype(jnp.bfloat16)
    if not last:
        outs[2][...] = state
        put_message(outs[0], half, state)


def feats_kernel(frac_ref, emb_ref, w_ref, after_ref, out_ref):
    del after_ref
    rows, cols, parts, atoms = frac_ref.shape
    feats = jnp.dot(emb_ref[...], w_ref[...], preferred_element_type=jnp.float32).astype(jnp.bfloat16)
    for r in range(rows):
        for c in range(cols):
            at = (r * cols + c) * atoms
            out_ref[r, c, 0:atoms, :] = feats[at : at + atoms]
            f = frac_ref[r, c].astype(jnp.float32)
            f = jnp.concatenate([f, jnp.zeros((FRAC_ROWS - parts, atoms), jnp.float32)], axis=0)
            out_ref[r, c, atoms : atoms + FRAC_ROWS, :] = f.astype(jnp.bfloat16)


def pair_kernel(first, codes_ref, ext_ref, got_ref, mix_ref, after_ref, out_ref, near3, fields, basis, gathered):
    del after_ref
    rows, width, packed, channels = ext_ref.shape
    atoms = packed - FRAC_ROWS
    cols = width - 2
    npb = codes_ref.shape[-1]
    nrbf = mix_ref.shape[0]
    core = lax.rem(lax.axis_index("gx"), 2)
    above = core if first else 1 - core
    row = 1 - above

    @pl.when(above == 0)
    def _():
        near3[0:rows] = ext_ref[...]
        near3[rows] = got_ref[...]

    @pl.when(above == 1)
    def _():
        near3[0] = got_ref[...]
        near3[1 : rows + 1] = ext_ref[...]

    for r in range(rows + 1):
        for c in range(width):
            fields[r * width + c] = near3[r, c, atoms:packed, :].astype(jnp.float32)[0:8]

    order = lax.broadcasted_iota(jnp.int32, (nrbf, channels), 0).astype(jnp.float32) - nrbf // 2
    mix = mix_ref[...] * (jnp.exp(-order * order) * MSG_SCALE)
    bits = math.sqrt(math.log2(math.e))

    for c in range(cols):
        own = fields[width + c + 1]
        own = jnp.transpose(jnp.concatenate([own] * (LANES // 8), axis=0))
        own_x = jnp.broadcast_to(own[:, 0:1], (atoms, atoms))
        own_y = jnp.broadcast_to(own[:, 1:2], (atoms, atoms))
        own_z = jnp.broadcast_to(own[:, 2:3] * (HEIGHT / CELL), (atoms, atoms))
        slot = c % 2
        for p in range(npb):
            code = codes_ref[row, c, p]
            step_x, step_y = code // 3 - 1, code % 3 - 1
            near = fields[(1 + step_x) * width + c + 1 + step_y]
            dx = (near[0:1] + step_x.astype(jnp.float32)) - own_x
            dy = (near[1:2] + step_y.astype(jnp.float32)) - own_y
            dz = jnp.abs(near[2:3] * (HEIGHT / CELL) - own_z)
            dz = jnp.minimum(dz, HEIGHT / CELL - dz)
            s = jnp.minimum(dx * dx + dy * dy + dz * dz, 1.0)
            root = s * lax.rsqrt(jnp.maximum(s, 1e-30))
            z = root * (bits * (nrbf - 1)) - bits * (nrbf // 2)
            env = (1.0 - s) * horner(ENV_POLY, s)
            mid = env * env * jnp.exp2(-(z * z))
            up, down = jnp.exp2((2.0 * bits) * z), jnp.exp2((-2.0 * bits) * z)
            at = slice(p * atoms, (p + 1) * atoms)
            value = mid
            for q in range(nrbf // 2, nrbf):
                basis[slot, q * atoms : (q + 1) * atoms, at] = value.astype(jnp.bfloat16)
                value = value * up
            value = mid
            for q in range(nrbf // 2 - 1, -1, -1):
                value = value * down
                basis[slot, q * atoms : (q + 1) * atoms, at] = value.astype(jnp.bfloat16)
            gathered[slot, at, :] = near3[1 + step_x, c + 1 + step_y, 0:atoms, :]
        parts = jnp.dot(basis[slot], gathered[slot], preferred_element_type=jnp.float32)
        total = parts[0:atoms] * mix[0:1]
        for q in range(1, nrbf):
            total = total + parts[q * atoms : (q + 1) * atoms] * mix[q : q + 1]
        out_ref[c] = total


def field_part(scale, half_ref, weight_ref, w_ref, table_ref):
    w_t = jnp.transpose(w_ref[...].astype(jnp.float32)).astype(jnp.bfloat16)
    factors = lax.dot_general(w_t, half_ref[...], (((1,), (1,)), ((), ())), preferred_element_type=jnp.float32)
    factors = (factors * (weight_ref[...] * scale)).astype(jnp.bfloat16)
    return jnp.dot(factors, table_ref[...], preferred_element_type=jnp.float32)


def own_field_kernel(scale, half_ref, weight_ref, w_ref, table_ref, emb_ref, msg1_ref, msg2_ref, out_ref):
    cols, atoms, _ = msg1_ref.shape
    row1 = 1 - lax.rem(lax.axis_index("gx"), 2)
    total = field_part(scale, half_ref, weight_ref, w_ref, table_ref)
    for r in range(2):
        for c in range(cols):
            i = r * cols + c
            at = slice(i * atoms, (i + 1) * atoms)
            msg = jnp.where(row1 == r, msg1_ref[c], msg2_ref[c])
            out_ref[i] = emb_ref[at, :].astype(jnp.float32) + msg + jnp.transpose(total[:, at])


def other_field_kernel(scale, half_ref, weight_ref, w_ref, table_ref, part_ref, out_ref, done, sems):
    cells, atoms, _ = done.shape
    total = field_part(scale, half_ref, weight_ref, w_ref, table_ref)
    copies = []
    for i in range(cells):
        done[i] = part_ref[i] + jnp.transpose(total[:, i * atoms : (i + 1) * atoms])
        copy = pltpu.make_async_copy(done.at[i], out_ref.at[i], sems.at[i])
        copy.start()
        copies.append(copy)
    for copy in copies:
        copy.wait()


def vmem(count):
    return [pl.BlockSpec(memory_space=pltpu.VMEM)] * count


def shards(embed, frac, pair_blocks, w_in, rbf_mix, w_charge, k_index, k_weight):
    f32, bf16 = jnp.float32, jnp.bfloat16
    rows, cols, atoms, channels = embed.shape
    kvec = k_weight.shape[0]
    npb = pair_blocks.shape[-1]
    nrbf = rbf_mix.shape[0]
    size_x, size_y = lax.axis_size("gx"), lax.axis_size("gy")
    count = size_x * size_y
    cells = rows * cols
    width = cols + 2
    flat = embed.reshape(-1, channels)
    unread = [pl.BlockSpec(memory_space=pl.ANY)]

    def call(body, name, ins, outs, scratch=(), smem=0, after=None, us=1.0, out_space=pltpu.VMEM):
        specs = [pl.BlockSpec(memory_space=pltpu.SMEM)] * smem + vmem(len(ins) - smem)
        if after is not None:
            ins, specs = [*ins, after], specs + unread
        return pl.pallas_call(
            body,
            out_shape=[jax.ShapeDtypeStruct(*o) for o in outs],
            in_specs=specs,
            out_specs=[pl.BlockSpec(memory_space=out_space)] * len(outs),
            scratch_shapes=[pltpu.VMEM(*s) if isinstance(s, tuple) else s for s in scratch],
            compiler_params=pltpu.CompilerParams(vmem_limit_bytes=32 * MIB),
            cost_estimate=pl.CostEstimate(flops=int(us * 1.15e9), bytes_accessed=0, transcendentals=0),
            name=name,
        )(*ins)

    def exchange(values, mask_of):
        return lax.ppermute(values, ("gx", "gy"), [(i, i ^ mask_of(i)) for i in range(count)])

    acc_out, state_out = ((kvec, channels), f32), ((8, LANES), f32)
    send_out = ((kvec + TAIL, channels), bf16)
    table_out = ((kvec, cells * atoms), bf16)
    k16, x16 = ((16, kvec), f32), ((16, cells * atoms), f32)
    shape = (rows * size_x, cols * size_y)
    table_theirs, send = call(
        functools.partial(tables_kernel, True, *shape), "sent_half",
        [frac, k_index, flat], [table_out, send_out], [k16, x16, state_out], after=k_weight, us=2.5,
    )
    table_mine, acc, state = call(
        functools.partial(tables_kernel, False, *shape), "kept_half",
        [frac, k_index, flat], [table_out, acc_out, state_out], [k16, x16], after=table_theirs, us=2.5,
    )

    def merge(acc, state, got, after, last=False):
        outs = [((kvec, channels), bf16)] if last else [send_out, acc_out, state_out]
        return call(functools.partial(merge_kernel, last), "merge", [acc, state, got], outs, after=after, us=5.0)

    core_bit = size_y
    along_y = [1 << b for b in range(size_y.bit_length() - 1)]
    along_x = [core_bit << b for b in range(1, size_x.bit_length() - 1)]
    masks = [along_x[1], *along_y, along_x[0], *along_x[2:]]
    swapped = [along_x[0], *along_y, *along_x[2:], along_x[1]]

    def cross(send, t):
        return exchange(send, lambda i: swapped[t] if i & core_bit else masks[t])

    send, acc, state = merge(acc, state, exchange(send, lambda i: core_bit), table_mine)

    got = cross(send, 0)
    (packed,) = call(
        feats_kernel, "feats", [frac, flat, w_in], [((rows, cols, atoms + FRAC_ROWS, channels), bf16)], after=state
    )
    if size_y == 2:
        edges = lax.ppermute(jnp.stack([packed[:, -1], packed[:, 0]], axis=1), "gy", [(0, 1), (1, 0)])
        west, east = edges[:, 0:1], edges[:, 1:2]
    else:
        west = lax.ppermute(packed[:, -1:], "gy", [(i, (i + 1) % size_y) for i in range(size_y)])
        east = lax.ppermute(packed[:, :1], "gy", [((i + 1) % size_y, i) for i in range(size_y)])
    send, acc, state = merge(acc, state, got, packed)

    got = cross(send, 1)
    ext = jnp.concatenate([west, packed, east], axis=1)
    core = lax.rem(lax.axis_index("gx"), 2)
    toward_1 = lax.dynamic_index_in_dim(ext, 1 - core, 0, keepdims=False)
    toward_2 = lax.dynamic_index_in_dim(ext, core, 0, keepdims=False)
    got_1 = lax.ppermute(toward_1, "gx", [(i, i ^ 1) for i in range(size_x)])
    got_2 = lax.ppermute(
        toward_2, "gx", [(i, (i - 1) % size_x if i % 2 == 0 else (i + 1) % size_x) for i in range(size_x)]
    )
    send, acc, state = merge(acc, state, got, ext)

    def pairs(first, got_row, after):
        (out,) = call(
            functools.partial(pair_kernel, first), "pairs",
            [pair_blocks, ext, got_row, rbf_mix], [((cols, atoms, channels), f32)],
            [
                ((rows + 1, width, atoms + FRAC_ROWS, channels), bf16),
                (((rows + 1) * width, 8, atoms), f32),
                ((2, nrbf * atoms, npb * atoms), bf16),
                ((2, npb * atoms, channels), bf16),
            ],
            smem=1, after=after, us=4.0,
        )
        return out

    messages = [None, None]
    for t in range(2, len(masks)):
        got = cross(send, t)
        after = state
        if t < 4:
            after = messages[t - 2] = pairs(t == 2, got_1 if t == 2 else got_2, state)
        if t < len(masks) - 1:
            send, acc, state = merge(acc, state, got, after)
    (mine,) = merge(acc, state, got, after, last=True)
    theirs = exchange(mine, lambda i: core_bit)

    scale = 1.0 / math.sqrt(cells * count * atoms * kvec)
    weight = k_weight.reshape(1, kvec)
    out = ((cells, atoms, channels), f32)
    (part,) = call(
        functools.partial(own_field_kernel, scale), "own_field",
        [mine, weight, w_charge, table_mine, flat, *messages], [out],
    )
    (updated,) = call(
        functools.partial(other_field_kernel, scale), "other_field",
        [theirs, weight, w_charge, table_theirs, part], [out], [out, pltpu.SemaphoreType.DMA((cells,))],
        out_space=pl.ANY,
    )
    return updated.reshape(embed.shape)


def solution(mesh):
    in_specs = (
        P("gx", "gy", None, None),
        P("gx", "gy", None, None),
        P("gx", "gy", None),
        P(),
        P(),
        P(),
        P(),
        P(),
    )
    out_specs = P("gx", "gy", None, None)
    return jax.shard_map(shards, mesh=mesh, in_specs=in_specs, out_specs=out_specs, check_vma=False)
```

```python
import functools
import math

import jax
import jax.numpy as jnp
from jax import lax
from jax.experimental import pallas as pl
from jax.experimental.pallas import tpu as pltpu
from jax.sharding import PartitionSpec as P

CELL = 5.0
HEIGHT = 51.2
MSG_SCALE = 0.5
LANES = 128
FRAC_ROWS = 16
TAIL = 32
MIB = 1024 * 1024

COS_POLY = (0.9999992251396179, -19.738981246948242, 64.92865753173828, -85.27162170410156, 58.79049301147461, -21.07110595703125)
SIN_POLY = (6.283185005187988, -41.341590881347656, 81.59994506835938, -76.61447143554688, 41.3428840637207, -12.471243858337402)
ENV_POLY = (0.9999998211860657, -0.23369461297988892, 0.019939105957746506, -0.000846334092784673)


def horner(coefs, s):
    acc = coefs[-1] * s + coefs[-2]
    for c in coefs[-3::-1]:
        acc = acc * s + c
    return acc


def pieces(x):
    hi = x.astype(jnp.bfloat16).astype(jnp.float32)
    rest = x - hi
    mid = rest.astype(jnp.bfloat16).astype(jnp.float32)
    return hi, mid, rest - mid


def stack(rows, order):
    row = lax.broadcasted_iota(jnp.int32, (16, LANES), 0)
    out = jnp.zeros((16, LANES), jnp.float32)
    for at, which in enumerate(order):
        out = jnp.where(row == at, jnp.broadcast_to(rows[which], (16, LANES)), out)
    return out.astype(jnp.bfloat16)


def outer_row(column, row):
    return lax.dot_general(
        stack(column, (0, 0, 0, 1, 1, 2)), row, (((0,), (0,)), ((), ())), preferred_element_type=jnp.float32
    )


def row_stack(row):
    return stack(pieces(row), (0, 1, 2, 0, 1, 0))


def put_message(send_ref, half, state):
    parts = [*pieces(state), jnp.zeros_like(state)]
    send_ref[half : half + TAIL, :] = jnp.concatenate(parts, axis=0).astype(jnp.bfloat16)


def half_table(half, k16, x16, sums_rhs, mean, state_ref, table_ref, store):
    kvec = table_ref.shape[0]
    nb = kvec // LANES
    offset = half.astype(jnp.float32) * 0.25
    state_ref[...] = jnp.zeros_like(state_ref)
    state_ref[nb : nb + 1, :] = mean
    for b in range(nb):
        at = slice(b * LANES, (b + 1) * LANES)
        turns = lax.dot_general(k16[:, at], x16, (((0,), (0,)), ((), ())), preferred_element_type=jnp.float32)
        turns = turns - offset
        turns = turns - jnp.round(turns)
        table = horner(COS_POLY, turns * turns).astype(jnp.bfloat16)
        table_ref[at, :] = table
        total = jnp.dot(table, sums_rhs(), preferred_element_type=jnp.float32)
        count = total[:, LANES:]
        state_ref[b : b + 1, :] = jnp.transpose(count)[0:1]
        store(at, total[:, :LANES] - count * mean)


def sent_kernel(
    nx, ny, frac_hbm, kidx_hbm, emb_hbm, table_ref, send_ref, k16_ref, x16_ref, rhs, mean_ref, frac_ref,
    kf32, xf32, state, kidx_ref, sems,
):
    rows, _, cols, atoms = frac_ref.shape
    kvec = kidx_ref.shape[1]
    n = rows * cols * atoms
    fetches = [
        pltpu.make_async_copy(kidx_hbm, kidx_ref, sems.at[0]),
        pltpu.make_async_copy(frac_hbm, frac_ref, sems.at[1]),
        pltpu.make_async_copy(emb_hbm, rhs.at[:, 0:LANES], sems.at[2]),
    ]
    for fetch in fetches:
        fetch.start()
    me_x, me_y = lax.axis_index("gx"), lax.axis_index("gy")
    kf32[...] = jnp.zeros_like(kf32)
    xf32[...] = jnp.zeros_like(xf32)
    rhs[:, LANES:] = jnp.ones((n, LANES), jnp.bfloat16)
    fetches[0].wait()
    fetches[1].wait()
    kf = kidx_ref[...].astype(jnp.float32)
    kf32[0:1, :] = kf[0:1] * (1.0 / nx)
    kf32[1:2, :] = kf[0:1] * (1.0 / nx)
    kf32[2:3, :] = kf[1:2] * (1.0 / ny)
    kf32[3:4, :] = kf[1:2] * (1.0 / ny)
    kf32[4:5, :] = kf[2:3]
    for r in range(rows):
        f = [frac_ref[r, q].astype(jnp.float32) for q in range(3)]
        for c in range(cols):
            at = slice((r * cols + c) * atoms, (r * cols + c + 1) * atoms)
            xf32[0:1, at] = jnp.full((1, atoms), me_x * rows + r, jnp.int32).astype(jnp.float32)
            xf32[1:2, at] = f[0][c : c + 1]
            xf32[2:3, at] = jnp.full((1, atoms), me_y * cols + c, jnp.int32).astype(jnp.float32)
            xf32[3:4, at] = f[1][c : c + 1]
            xf32[4:5, at] = f[2][c : c + 1]
    k16 = kf32[...].astype(jnp.bfloat16)
    x16 = xf32[...].astype(jnp.bfloat16)
    k16_ref[...] = k16
    x16_ref[...] = x16
    fetches[2].wait()
    mean = jnp.sum(rhs[:, 0:LANES].astype(jnp.float32), axis=0, keepdims=True) * (1.0 / n)
    mean_ref[...] = jnp.broadcast_to(mean, mean_ref.shape)

    def store(at, centred):
        send_ref[at, :] = centred.astype(jnp.bfloat16)

    half_table(1 - lax.rem(me_x, 2), k16, x16, lambda: rhs[...], mean, state, table_ref, store)
    put_message(send_ref, kvec, state[...])


def kept_kernel(k16_ref, x16_ref, rhs_ref, mean_ref, table_ref, acc_ref, state_ref):
    def store(at, centred):
        acc_ref[at, :] = centred

    core = lax.rem(lax.axis_index("gx"), 2)
    half_table(
        core, k16_ref[...], x16_ref[...], lambda: rhs_ref[...], mean_ref[0:1], state_ref, table_ref, store
    )


def merge_kernel(last, acc_ref, state_ref, got_ref, after_ref, *outs):
    del after_ref
    half = acc_ref.shape[0]
    nb = half // LANES
    tail = got_ref[half : half + TAIL, :].astype(jnp.float32)
    theirs = tail[0:8] + tail[8:16] + tail[16:24]
    mine = state_ref[...]
    weight = jnp.where(lax.broadcasted_iota(jnp.int32, (8, LANES), 0) < nb, 1.0, 0.5)
    state = (mine + theirs) * weight
    diff = (mine - theirs) * weight
    split = pieces(diff)
    means = row_stack(diff[nb : nb + 1])
    for b in range(nb):
        at = slice(b * LANES, (b + 1) * LANES)
        part = outer_row([piece[b : b + 1] for piece in split], means)
        merged = acc_ref[at, :] + got_ref[at, :].astype(jnp.float32) + part
        if not last:
            outs[1][at, :] = merged
        outs[0][at, :] = merged.astype(jnp.bfloat16)
    if not last:
        outs[2][...] = state
        put_message(outs[0], half, state)


def feats_kernel(scale, frac_ref, emb_ref, w_ref, charge_ref, weight_ref, after_ref, out_ref, charge_t_ref, scaled_ref):
    del after_ref
    rows, parts, cols, atoms = frac_ref.shape
    feats = jnp.dot(emb_ref[:, 0:LANES], w_ref[...], preferred_element_type=jnp.float32).astype(jnp.bfloat16)
    row = lax.broadcasted_iota(jnp.int32, (FRAC_ROWS, atoms), 0)
    for r in range(rows):
        f = [frac_ref[r, q].astype(jnp.float32) for q in range(parts)]
        for c in range(cols):
            at = (r * cols + c) * atoms
            out_ref[r, c, 0:atoms, :] = feats[at : at + atoms]
            packed = jnp.zeros((FRAC_ROWS, atoms), jnp.float32)
            for q in range(parts):
                packed = jnp.where(row == q, jnp.broadcast_to(f[q][c : c + 1], (FRAC_ROWS, atoms)), packed)
            out_ref[r, c, atoms : atoms + FRAC_ROWS, :] = packed.astype(jnp.bfloat16)
    charge_t_ref[...] = jnp.transpose(charge_ref[...].astype(jnp.float32)).astype(jnp.bfloat16)
    scaled_ref[...] = weight_ref[...] * scale


def pair_kernel(first, codes_ref, ext_ref, got_ref, mix_ref, after_ref, out_ref, near3, fields, basis, gathered):
    del after_ref
    rows, width, packed, channels = ext_ref.shape
    atoms = packed - FRAC_ROWS
    cols = width - 2
    npb = codes_ref.shape[-1]
    nrbf = mix_ref.shape[0]
    core = lax.rem(lax.axis_index("gx"), 2)
    above = core if first else 1 - core
    row = 1 - above

    @pl.when(above == 0)
    def _():
        near3[0:rows] = ext_ref[...]
        near3[rows] = got_ref[...]

    @pl.when(above == 1)
    def _():
        near3[0] = got_ref[...]
        near3[1 : rows + 1] = ext_ref[...]

    for r in range(rows + 1):
        for c in range(width):
            fields[r * width + c] = near3[r, c, atoms:packed, :].astype(jnp.float32)[0:8]

    order = lax.broadcasted_iota(jnp.int32, (nrbf, channels), 0).astype(jnp.float32) - nrbf // 2
    mix = mix_ref[...] * (jnp.exp(-order * order) * MSG_SCALE)
    bits = math.sqrt(math.log2(math.e))

    for c in range(cols):
        own = fields[width + c + 1]
        own = jnp.transpose(jnp.concatenate([own] * (LANES // 8), axis=0))
        own_x = jnp.broadcast_to(own[:, 0:1], (atoms, atoms))
        own_y = jnp.broadcast_to(own[:, 1:2], (atoms, atoms))
        own_z = jnp.broadcast_to(own[:, 2:3] * (HEIGHT / CELL), (atoms, atoms))
        slot = c % 2
        for p in range(npb):
            code = codes_ref[row, c, p]
            step_x, step_y = code // 3 - 1, code % 3 - 1
            near = fields[(1 + step_x) * width + c + 1 + step_y]
            dx = (near[0:1] + step_x.astype(jnp.float32)) - own_x
            dy = (near[1:2] + step_y.astype(jnp.float32)) - own_y
            dz = jnp.abs(near[2:3] * (HEIGHT / CELL) - own_z)
            dz = jnp.minimum(dz, HEIGHT / CELL - dz)
            s = jnp.minimum(dx * dx + dy * dy + dz * dz, 1.0)
            root = s * lax.rsqrt(jnp.maximum(s, 1e-30))
            z = root * (bits * (nrbf - 1)) - bits * (nrbf // 2)
            env = (1.0 - s) * horner(ENV_POLY, s)
            mid = env * env * jnp.exp2(-(z * z))
            up, down = jnp.exp2((2.0 * bits) * z), jnp.exp2((-2.0 * bits) * z)
            at = slice(p * atoms, (p + 1) * atoms)
            value = mid
            for q in range(nrbf // 2, nrbf):
                basis[slot, q * atoms : (q + 1) * atoms, at] = value.astype(jnp.bfloat16)
                value = value * up
            value = mid
            for q in range(nrbf // 2 - 1, -1, -1):
                value = value * down
                basis[slot, q * atoms : (q + 1) * atoms, at] = value.astype(jnp.bfloat16)
            gathered[slot, at, :] = near3[1 + step_x, c + 1 + step_y, 0:atoms, :]
        parts = jnp.dot(basis[slot], gathered[slot], preferred_element_type=jnp.float32)
        total = parts[0:atoms] * mix[0:1]
        for q in range(1, nrbf):
            total = total + parts[q * atoms : (q + 1) * atoms] * mix[q : q + 1]
        out_ref[c] = total


def field_part(half_ref, weight_ref, charge_t_ref, table_ref):
    factors = lax.dot_general(
        charge_t_ref[...], half_ref[...], (((1,), (1,)), ((), ())), preferred_element_type=jnp.float32
    )
    factors = (factors * weight_ref[...]).astype(jnp.bfloat16)
    return jnp.dot(factors, table_ref[...], preferred_element_type=jnp.float32)


def own_field_kernel(half_ref, weight_ref, charge_t_ref, table_ref, emb_ref, msg1_ref, msg2_ref, out_ref):
    cols, atoms, _ = msg1_ref.shape
    row1 = 1 - lax.rem(lax.axis_index("gx"), 2)
    total = field_part(half_ref, weight_ref, charge_t_ref, table_ref)
    for r in range(2):
        for c in range(cols):
            i = r * cols + c
            at = slice(i * atoms, (i + 1) * atoms)
            msg = jnp.where(row1 == r, msg1_ref[c], msg2_ref[c])
            out_ref[i] = emb_ref[at, 0:LANES].astype(jnp.float32) + msg + jnp.transpose(total[:, at])


def other_field_kernel(half_ref, weight_ref, charge_t_ref, table_ref, part_ref, out_ref, done, sems):
    cells, atoms, _ = done.shape
    total = field_part(half_ref, weight_ref, charge_t_ref, table_ref)
    copies = []
    for i in range(cells):
        done[i] = part_ref[i] + jnp.transpose(total[:, i * atoms : (i + 1) * atoms])
        copy = pltpu.make_async_copy(done.at[i], out_ref.at[i], sems.at[i])
        copy.start()
        copies.append(copy)
    for copy in copies:
        copy.wait()


def in_hbm(x):
    return pltpu.with_memory_space_constraint(x, pltpu.HBM)


def vmem(count):
    return [pl.BlockSpec(memory_space=pltpu.VMEM)] * count


def shards(embed, frac, pair_blocks, w_in, rbf_mix, w_charge, k_index, k_weight):
    f32, bf16 = jnp.float32, jnp.bfloat16
    rows, cols, atoms, channels = embed.shape
    kvec = k_weight.shape[0]
    npb = pair_blocks.shape[-1]
    nrbf = rbf_mix.shape[0]
    size_x, size_y = lax.axis_size("gx"), lax.axis_size("gy")
    count = size_x * size_y
    cells = rows * cols
    width = cols + 2
    unread = [pl.BlockSpec(memory_space=pl.ANY)]

    def call(body, name, ins, outs, scratch=(), smem=0, after=None, us=1.0, out_space=pltpu.VMEM, hbm=0):
        specs = [pl.BlockSpec(memory_space=pltpu.SMEM)] * smem + vmem(len(ins) - smem - hbm)
        specs += [pl.BlockSpec(memory_space=pltpu.HBM)] * hbm
        if after is not None:
            ins, specs = [*ins, after], specs + unread
        return pl.pallas_call(
            body,
            out_shape=[jax.ShapeDtypeStruct(*o) for o in outs],
            in_specs=specs,
            out_specs=[pl.BlockSpec(memory_space=out_space)] * len(outs),
            scratch_shapes=[pltpu.VMEM(*s) if isinstance(s, tuple) else s for s in scratch],
            compiler_params=pltpu.CompilerParams(vmem_limit_bytes=32 * MIB),
            cost_estimate=pl.CostEstimate(flops=int(us * 1.15e9), bytes_accessed=0, transcendentals=0),
            name=name,
        )(*ins)

    def exchange(values, mask_of):
        return lax.ppermute(values, ("gx", "gy"), [(i, i ^ mask_of(i)) for i in range(count)])

    acc_out, state_out = ((kvec, channels), f32), ((8, LANES), f32)
    send_out = ((kvec + TAIL, channels), bf16)
    table_out = ((kvec, cells * atoms), bf16)
    k16, x16 = (16, kvec), (16, cells * atoms)
    table_theirs, send, *operands, parts = call(
        functools.partial(sent_kernel, rows * size_x, cols * size_y), "sent_half",
        [in_hbm(jnp.transpose(frac, (0, 2, 1, 3))), in_hbm(k_index), in_hbm(embed.reshape(-1, channels))],
        [table_out, send_out, (k16, bf16), (x16, bf16), ((cells * atoms, 2 * LANES), bf16), state_out,
         ((rows, frac.shape[2], cols, atoms), bf16)],
        [(k16, f32), (x16, f32), state_out, (k_index.shape, jnp.int32), pltpu.SemaphoreType.DMA((3,))],
        hbm=3, us=2.5,
    )
    embedded = operands[2]
    table_mine, acc, state = call(kept_kernel, "kept_half", operands, [table_out, acc_out, state_out], us=2.5)

    def merge(acc, state, got, after, last=False):
        outs = [((kvec, channels), bf16)] if last else [send_out, acc_out, state_out]
        return call(functools.partial(merge_kernel, last), "merge", [acc, state, got], outs, after=after, us=5.0)

    core_bit = size_y
    along_y = [1 << b for b in range(size_y.bit_length() - 1)]
    along_x = [core_bit << b for b in range(1, size_x.bit_length() - 1)]
    masks = [along_x[1], along_x[0], *along_y, *along_x[2:]]
    swapped = [along_x[0], *along_x[2:], *along_y, along_x[1]]

    def cross(send, t):
        return exchange(send, lambda i: swapped[t] if i & core_bit else masks[t])

    send, acc, state = merge(acc, state, exchange(send, lambda i: core_bit), table_mine)

    got = cross(send, 0)
    packed, charge_t, weight = call(
        functools.partial(feats_kernel, 1.0 / math.sqrt(cells * count * atoms * kvec)), "feats",
        [parts, embedded, w_in, w_charge, k_weight.reshape(1, kvec)],
        [((rows, cols, atoms + FRAC_ROWS, channels), bf16), (w_charge.shape, bf16), ((1, kvec), f32)], after=state,
    )
    if size_y == 2:
        edges = lax.ppermute(jnp.stack([packed[:, -1], packed[:, 0]], axis=1), "gy", [(0, 1), (1, 0)])
        west, east = edges[:, 0:1], edges[:, 1:2]
    else:
        west = lax.ppermute(packed[:, -1:], "gy", [(i, (i + 1) % size_y) for i in range(size_y)])
        east = lax.ppermute(packed[:, :1], "gy", [((i + 1) % size_y, i) for i in range(size_y)])
    send, acc, state = merge(acc, state, got, packed)

    got = cross(send, 1)
    ext = jnp.concatenate([west, packed, east], axis=1)
    core = lax.rem(lax.axis_index("gx"), 2)
    toward_1 = lax.dynamic_index_in_dim(ext, 1 - core, 0, keepdims=False)
    toward_2 = lax.dynamic_index_in_dim(ext, core, 0, keepdims=False)
    got_1 = lax.ppermute(toward_1, "gx", [(i, i ^ 1) for i in range(size_x)])
    got_2 = lax.ppermute(
        toward_2, "gx", [(i, (i - 1) % size_x if i % 2 == 0 else (i + 1) % size_x) for i in range(size_x)]
    )
    send, acc, state = merge(acc, state, got, ext)

    def pairs(first, got_row, after):
        (out,) = call(
            functools.partial(pair_kernel, first), "pairs",
            [pair_blocks, ext, got_row, rbf_mix], [((cols, atoms, channels), f32)],
            [
                ((rows + 1, width, atoms + FRAC_ROWS, channels), bf16),
                (((rows + 1) * width, 8, atoms), f32),
                ((2, nrbf * atoms, npb * atoms), bf16),
                ((2, npb * atoms, channels), bf16),
            ],
            smem=1, after=after, us=4.0,
        )
        return out

    messages = [None, None]
    for t in range(2, len(masks)):
        got = cross(send, t)
        after = state
        if t < 4:
            after = messages[t - 2] = pairs(t == 2, got_1 if t == 2 else got_2, state)
        if t < len(masks) - 1:
            send, acc, state = merge(acc, state, got, after)
    (mine,) = merge(acc, state, got, after, last=True)
    theirs = exchange(mine, lambda i: core_bit)

    out = ((cells, atoms, channels), f32)
    (part,) = call(
        own_field_kernel, "own_field", [mine, weight, charge_t, table_mine, embedded, *messages], [out]
    )
    (updated,) = call(
        other_field_kernel, "other_field", [theirs, weight, charge_t, table_theirs, part], [out],
        [out, pltpu.SemaphoreType.DMA((cells,))], out_space=pl.ANY,
    )
    return updated.reshape(embed.shape)


def solution(mesh):
    in_specs = (
        P("gx", "gy", None, None),
        P("gx", "gy", None, None),
        P("gx", "gy", None),
        P(),
        P(),
        P(),
        P(),
        P(),
    )
    out_specs = P("gx", "gy", None, None)
    return jax.shard_map(shards, mesh=mesh, in_specs=in_specs, out_specs=out_specs, check_vma=False)
```

```python
import functools
import math

import jax
import jax.numpy as jnp
from jax import lax
from jax.experimental import pallas as pl
from jax.experimental.pallas import tpu as pltpu
from jax.sharding import PartitionSpec as P

CELL = 5.0
HEIGHT = 51.2
MSG_SCALE = 0.5
LANES = 128
FRAC_ROWS = 16
TAIL = 32
MIB = 1024 * 1024

COS_POLY = (0.9999992251396179, -19.738981246948242, 64.92865753173828, -85.27162170410156, 58.79049301147461, -21.07110595703125)
SIN_POLY = (6.283185005187988, -41.341590881347656, 81.59994506835938, -76.61447143554688, 41.3428840637207, -12.471243858337402)
ENV_POLY = (0.9999998211860657, -0.23369461297988892, 0.019939105957746506, -0.000846334092784673)


def horner(coefs, s):
    acc = coefs[-1] * s + coefs[-2]
    for c in coefs[-3::-1]:
        acc = acc * s + c
    return acc


def pieces(x):
    hi = x.astype(jnp.bfloat16).astype(jnp.float32)
    rest = x - hi
    mid = rest.astype(jnp.bfloat16).astype(jnp.float32)
    return hi, mid, rest - mid


def stack(rows, order):
    row = lax.broadcasted_iota(jnp.int32, (16, LANES), 0)
    out = jnp.zeros((16, LANES), jnp.float32)
    for at, which in enumerate(order):
        out = jnp.where(row == at, jnp.broadcast_to(rows[which], (16, LANES)), out)
    return out.astype(jnp.bfloat16)


def outer_row(column, row):
    return lax.dot_general(
        stack(column, (0, 0, 0, 1, 1, 2)), row, (((0,), (0,)), ((), ())), preferred_element_type=jnp.float32
    )


def row_stack(row):
    return stack(pieces(row), (0, 1, 2, 0, 1, 0))


def put_message(send_ref, half, state):
    parts = [*pieces(state), jnp.zeros_like(state)]
    send_ref[half : half + TAIL, :] = jnp.concatenate(parts, axis=0).astype(jnp.bfloat16)


def half_table(half, k16, x16, sums_rhs, mean, state_ref, table_ref, store):
    kvec = table_ref.shape[0]
    nb = kvec // LANES
    offset = half.astype(jnp.float32) * 0.25
    state_ref[...] = jnp.zeros_like(state_ref)
    state_ref[nb : nb + 1, :] = mean
    block = min(kvec, 128)
    for start in range(0, kvec, block):
        at = slice(start, start + block)
        turns = lax.dot_general(k16[:, at], x16, (((0,), (0,)), ((), ())), preferred_element_type=jnp.float32)
        turns = turns - offset
        turns = turns - jnp.round(turns)
        table = horner(COS_POLY, turns * turns).astype(jnp.bfloat16)
        table_ref[at, :] = table
        total = jnp.dot(table, sums_rhs(), preferred_element_type=jnp.float32)
        count = total[:, LANES:]
        for b in range(block // LANES):
            part = jnp.transpose(count[b * LANES : (b + 1) * LANES])[0:1]
            state_ref[start // LANES + b : start // LANES + b + 1, :] = part
        store(at, total[:, :LANES] - count * mean)


def sent_kernel(
    nx, ny, frac_hbm, kidx_hbm, emb_hbm, in_hbm, charge_hbm, weight_hbm,
    table_ref, send_ref, k16_ref, x16_ref, rhs, mean_ref, frac_ref, in_ref, charge_ref, weight_ref,
    kf32, xf32, state, kidx_ref, sems,
):
    rows, _, cols, atoms = frac_ref.shape
    kvec = kidx_ref.shape[1]
    n = rows * cols * atoms
    fetches = [
        pltpu.make_async_copy(kidx_hbm, kidx_ref, sems.at[0]),
        pltpu.make_async_copy(frac_hbm, frac_ref, sems.at[1]),
        pltpu.make_async_copy(emb_hbm, rhs.at[:, 0:LANES], sems.at[2]),
        pltpu.make_async_copy(in_hbm, in_ref, sems.at[3]),
        pltpu.make_async_copy(charge_hbm, charge_ref, sems.at[4]),
        pltpu.make_async_copy(weight_hbm, weight_ref, sems.at[5]),
    ]
    for fetch in fetches:
        fetch.start()
    me_x, me_y = lax.axis_index("gx"), lax.axis_index("gy")
    kf32[...] = jnp.zeros_like(kf32)
    xf32[...] = jnp.zeros_like(xf32)
    rhs[:, LANES:] = jnp.ones((n, LANES), jnp.bfloat16)
    fetches[0].wait()
    fetches[1].wait()
    kf = kidx_ref[...].astype(jnp.float32)
    kf32[0:1, :] = kf[0:1] * (1.0 / nx)
    kf32[1:2, :] = kf[0:1] * (1.0 / nx)
    kf32[2:3, :] = kf[1:2] * (1.0 / ny)
    kf32[3:4, :] = kf[1:2] * (1.0 / ny)
    kf32[4:5, :] = kf[2:3]
    for r in range(rows):
        f = [frac_ref[r, q].astype(jnp.float32) for q in range(3)]
        for c in range(cols):
            at = slice((r * cols + c) * atoms, (r * cols + c + 1) * atoms)
            xf32[0:1, at] = jnp.full((1, atoms), me_x * rows + r, jnp.int32).astype(jnp.float32)
            xf32[1:2, at] = f[0][c : c + 1]
            xf32[2:3, at] = jnp.full((1, atoms), me_y * cols + c, jnp.int32).astype(jnp.float32)
            xf32[3:4, at] = f[1][c : c + 1]
            xf32[4:5, at] = f[2][c : c + 1]
    k16 = kf32[...].astype(jnp.bfloat16)
    x16 = xf32[...].astype(jnp.bfloat16)
    k16_ref[...] = k16
    x16_ref[...] = x16
    fetches[2].wait()
    mean = jnp.sum(rhs[:, 0:LANES].astype(jnp.float32), axis=0, keepdims=True) * (1.0 / n)
    mean_ref[...] = jnp.broadcast_to(mean, mean_ref.shape)

    def store(at, centred):
        send_ref[at, :] = centred.astype(jnp.bfloat16)

    half_table(1 - lax.rem(me_x, 2), k16, x16, lambda: rhs[...], mean, state, table_ref, store)
    put_message(send_ref, kvec, state[...])
    for fetch in fetches[3:]:
        fetch.wait()


def kept_kernel(k16_ref, x16_ref, rhs_ref, mean_ref, table_ref, acc_ref, state_ref):
    def store(at, centred):
        acc_ref[at, :] = centred

    core = lax.rem(lax.axis_index("gx"), 2)
    half_table(
        core, k16_ref[...], x16_ref[...], lambda: rhs_ref[...], mean_ref[0:1], state_ref, table_ref, store
    )


def merge_kernel(last, acc_ref, state_ref, got_ref, after_ref, *outs):
    del after_ref
    half = acc_ref.shape[0]
    nb = half // LANES
    tail = got_ref[half : half + TAIL, :].astype(jnp.float32)
    theirs = tail[0:8] + tail[8:16] + tail[16:24]
    mine = state_ref[...]
    weight = jnp.where(lax.broadcasted_iota(jnp.int32, (8, LANES), 0) < nb, 1.0, 0.5)
    state = (mine + theirs) * weight
    diff = (mine - theirs) * weight
    split = pieces(diff)
    means = row_stack(diff[nb : nb + 1])
    for b in range(nb):
        at = slice(b * LANES, (b + 1) * LANES)
        part = outer_row([piece[b : b + 1] for piece in split], means)
        merged = acc_ref[at, :] + got_ref[at, :].astype(jnp.float32) + part
        if not last:
            outs[1][at, :] = merged
        outs[0][at, :] = merged.astype(jnp.bfloat16)
    if not last:
        outs[2][...] = state
        put_message(outs[0], half, state)


def feats_kernel(scale, frac_ref, emb_ref, w_ref, charge_ref, weight_ref, after_ref, out_ref, charge_t_ref, scaled_ref):
    del after_ref
    rows, parts, cols, atoms = frac_ref.shape
    feats = jnp.dot(emb_ref[:, 0:LANES], w_ref[...], preferred_element_type=jnp.float32).astype(jnp.bfloat16)
    row = lax.broadcasted_iota(jnp.int32, (FRAC_ROWS, atoms), 0)
    for r in range(rows):
        f = [frac_ref[r, q].astype(jnp.float32) for q in range(parts)]
        for c in range(cols):
            at = (r * cols + c) * atoms
            out_ref[r, c, 0:atoms, :] = feats[at : at + atoms]
            packed = jnp.zeros((FRAC_ROWS, atoms), jnp.float32)
            for q in range(parts):
                packed = jnp.where(row == q, jnp.broadcast_to(f[q][c : c + 1], (FRAC_ROWS, atoms)), packed)
            out_ref[r, c, atoms : atoms + FRAC_ROWS, :] = packed.astype(jnp.bfloat16)
    charge_t_ref[...] = jnp.transpose(charge_ref[...].astype(jnp.float32)).astype(jnp.bfloat16)
    scaled_ref[...] = weight_ref[...] * scale


def pair_kernel(first, codes_ref, ext_ref, got_ref, mix_ref, after_ref, out_ref, near3, fields, basis, gathered):
    del after_ref
    rows, width, packed, channels = ext_ref.shape
    atoms = packed - FRAC_ROWS
    cols = width - 2
    npb = codes_ref.shape[-1]
    nrbf = mix_ref.shape[0]
    core = lax.rem(lax.axis_index("gx"), 2)
    above = core if first else 1 - core
    row = 1 - above

    @pl.when(above == 0)
    def _():
        near3[0:rows] = ext_ref[...]
        near3[rows] = got_ref[...]

    @pl.when(above == 1)
    def _():
        near3[0] = got_ref[...]
        near3[1 : rows + 1] = ext_ref[...]

    for r in range(rows + 1):
        for c in range(width):
            fields[r * width + c] = near3[r, c, atoms:packed, :].astype(jnp.float32)[0:8]

    order = lax.broadcasted_iota(jnp.int32, (nrbf, channels), 0).astype(jnp.float32) - nrbf // 2
    mix = mix_ref[...] * (jnp.exp(-order * order) * MSG_SCALE)
    bits = math.sqrt(math.log2(math.e))

    for c in range(cols):
        own = fields[width + c + 1]
        own = jnp.transpose(jnp.concatenate([own] * (LANES // 8), axis=0))
        own_x = jnp.broadcast_to(own[:, 0:1], (atoms, atoms))
        own_y = jnp.broadcast_to(own[:, 1:2], (atoms, atoms))
        own_z = jnp.broadcast_to(own[:, 2:3] * (HEIGHT / CELL), (atoms, atoms))
        slot = c % 2
        for p in range(npb):
            code = codes_ref[row, c, p]
            step_x, step_y = code // 3 - 1, code % 3 - 1
            near = fields[(1 + step_x) * width + c + 1 + step_y]
            dx = (near[0:1] + step_x.astype(jnp.float32)) - own_x
            dy = (near[1:2] + step_y.astype(jnp.float32)) - own_y
            dz = jnp.abs(near[2:3] * (HEIGHT / CELL) - own_z)
            dz = jnp.minimum(dz, HEIGHT / CELL - dz)
            s = jnp.minimum(dx * dx + dy * dy + dz * dz, 1.0)
            root = s * lax.rsqrt(jnp.maximum(s, 1e-30))
            z = root * (bits * (nrbf - 1)) - bits * (nrbf // 2)
            env = (1.0 - s) * horner(ENV_POLY, s)
            mid = env * env * jnp.exp2(-(z * z))
            up, down = jnp.exp2((2.0 * bits) * z), jnp.exp2((-2.0 * bits) * z)
            at = slice(p * atoms, (p + 1) * atoms)
            value = mid
            for q in range(nrbf // 2, nrbf):
                basis[slot, q * atoms : (q + 1) * atoms, at] = value.astype(jnp.bfloat16)
                value = value * up
            value = mid
            for q in range(nrbf // 2 - 1, -1, -1):
                value = value * down
                basis[slot, q * atoms : (q + 1) * atoms, at] = value.astype(jnp.bfloat16)
            gathered[slot, at, :] = near3[1 + step_x, c + 1 + step_y, 0:atoms, :]
        parts = jnp.dot(basis[slot], gathered[slot], preferred_element_type=jnp.float32)
        total = parts[0:atoms] * mix[0:1]
        for q in range(1, nrbf):
            total = total + parts[q * atoms : (q + 1) * atoms] * mix[q : q + 1]
        out_ref[c] = total


def field_part(half_ref, weight_ref, charge_t_ref, table_ref):
    factors = lax.dot_general(
        charge_t_ref[...], half_ref[...], (((1,), (1,)), ((), ())), preferred_element_type=jnp.float32
    )
    factors = (factors * weight_ref[...]).astype(jnp.bfloat16)
    return jnp.dot(factors, table_ref[...], preferred_element_type=jnp.float32)


def own_field_kernel(half_ref, weight_ref, charge_t_ref, table_ref, emb_ref, msg1_ref, msg2_ref, out_ref):
    cols, atoms, _ = msg1_ref.shape
    row1 = 1 - lax.rem(lax.axis_index("gx"), 2)
    total = field_part(half_ref, weight_ref, charge_t_ref, table_ref)
    for r in range(2):
        for c in range(cols):
            i = r * cols + c
            at = slice(i * atoms, (i + 1) * atoms)
            msg = jnp.where(row1 == r, msg1_ref[c], msg2_ref[c])
            out_ref[i] = emb_ref[at, 0:LANES].astype(jnp.float32) + msg + jnp.transpose(total[:, at])


def other_field_kernel(half_ref, weight_ref, charge_t_ref, table_ref, part_ref, out_ref, done, sems):
    cells, atoms, _ = done.shape
    total = field_part(half_ref, weight_ref, charge_t_ref, table_ref)
    copies = []
    for i in range(cells):
        done[i] = part_ref[i] + jnp.transpose(total[:, i * atoms : (i + 1) * atoms])
        copy = pltpu.make_async_copy(done.at[i], out_ref.at[i], sems.at[i])
        copy.start()
        copies.append(copy)
    for copy in copies:
        copy.wait()


def in_hbm(x):
    return pltpu.with_memory_space_constraint(x, pltpu.HBM)


def vmem(count):
    return [pl.BlockSpec(memory_space=pltpu.VMEM)] * count


def shards(embed, frac, pair_blocks, w_in, rbf_mix, w_charge, k_index, k_weight):
    f32, bf16 = jnp.float32, jnp.bfloat16
    rows, cols, atoms, channels = embed.shape
    kvec = k_weight.shape[0]
    npb = pair_blocks.shape[-1]
    nrbf = rbf_mix.shape[0]
    size_x, size_y = lax.axis_size("gx"), lax.axis_size("gy")
    count = size_x * size_y
    cells = rows * cols
    width = cols + 2
    unread = [pl.BlockSpec(memory_space=pl.ANY)]

    def call(body, name, ins, outs, scratch=(), smem=0, after=None, us=1.0, out_space=pltpu.VMEM, hbm=0):
        specs = [pl.BlockSpec(memory_space=pltpu.SMEM)] * smem + vmem(len(ins) - smem - hbm)
        specs += [pl.BlockSpec(memory_space=pltpu.HBM)] * hbm
        if after is not None:
            ins, specs = [*ins, after], specs + unread
        return pl.pallas_call(
            body,
            out_shape=[jax.ShapeDtypeStruct(*o) for o in outs],
            in_specs=specs,
            out_specs=[pl.BlockSpec(memory_space=out_space)] * len(outs),
            scratch_shapes=[pltpu.VMEM(*s) if isinstance(s, tuple) else s for s in scratch],
            compiler_params=pltpu.CompilerParams(vmem_limit_bytes=32 * MIB),
            cost_estimate=pl.CostEstimate(flops=int(us * 1.15e9), bytes_accessed=0, transcendentals=0),
            name=name,
        )(*ins)

    def exchange(values, mask_of):
        return lax.ppermute(values, ("gx", "gy"), [(i, i ^ mask_of(i)) for i in range(count)])

    acc_out, state_out = ((kvec, channels), f32), ((8, LANES), f32)
    send_out = ((kvec + TAIL, channels), bf16)
    table_out = ((kvec, cells * atoms), bf16)
    k16, x16 = (16, kvec), (16, cells * atoms)
    table_theirs, send, k16_in, x16_in, embedded, mean, parts, w_near, charge_near, weight_near = call(
        functools.partial(sent_kernel, rows * size_x, cols * size_y), "sent_half",
        [
            in_hbm(x)
            for x in (
                jnp.transpose(frac, (0, 2, 1, 3)), k_index, embed.reshape(-1, channels), w_in, w_charge,
                k_weight.reshape(1, kvec),
            )
        ],
        [table_out, send_out, (k16, bf16), (x16, bf16), ((cells * atoms, 2 * LANES), bf16), state_out,
         ((rows, frac.shape[2], cols, atoms), bf16), (w_in.shape, bf16), (w_charge.shape, bf16), ((1, kvec), f32)],
        [(k16, f32), (x16, f32), state_out, (k_index.shape, jnp.int32), pltpu.SemaphoreType.DMA((6,))],
        hbm=6, us=2.5,
    )

    table_mine, acc, state = call(
        kept_kernel, "kept_half", [k16_in, x16_in, embedded, mean], [table_out, acc_out, state_out], us=2.5
    )

    def merge(acc, state, got, after, last=False):
        outs = [((kvec, channels), bf16)] if last else [send_out, acc_out, state_out]
        return call(functools.partial(merge_kernel, last), "merge", [acc, state, got], outs, after=after, us=5.0)

    core_bit = size_y
    along_y = [1 << b for b in range(size_y.bit_length() - 1)]
    along_x = [core_bit << b for b in range(1, size_x.bit_length() - 1)]
    masks = [along_x[0], *along_y, *along_x[:0:-1]]
    swapped = [*along_x[1:], along_x[0], *along_y]

    def cross(send, t):
        return exchange(send, lambda i: swapped[t] if i & core_bit else masks[t])

    send, acc, state = merge(acc, state, exchange(send, lambda i: core_bit), table_mine)

    got = cross(send, 0)
    packed, charge_t, weight = call(
        functools.partial(feats_kernel, 1.0 / math.sqrt(cells * count * atoms * kvec)), "feats",
        [parts, embedded, w_near, charge_near, weight_near],
        [((rows, cols, atoms + FRAC_ROWS, channels), bf16), (w_charge.shape, bf16), ((1, kvec), f32)], after=state,
    )
    if size_y == 2:
        edges = lax.ppermute(jnp.stack([packed[:, -1], packed[:, 0]], axis=1), "gy", [(0, 1), (1, 0)])
        west, east = edges[:, 0:1], edges[:, 1:2]
    else:
        west = lax.ppermute(packed[:, -1:], "gy", [(i, (i + 1) % size_y) for i in range(size_y)])
        east = lax.ppermute(packed[:, :1], "gy", [((i + 1) % size_y, i) for i in range(size_y)])
    send, acc, state = merge(acc, state, got, packed)

    got = cross(send, 1)
    ext = jnp.concatenate([west, packed, east], axis=1)
    core = lax.rem(lax.axis_index("gx"), 2)
    toward_1 = lax.dynamic_index_in_dim(ext, 1 - core, 0, keepdims=False)
    toward_2 = lax.dynamic_index_in_dim(ext, core, 0, keepdims=False)
    got_1 = lax.ppermute(toward_1, "gx", [(i, i ^ 1) for i in range(size_x)])
    got_2 = lax.ppermute(
        toward_2, "gx", [(i, (i - 1) % size_x if i % 2 == 0 else (i + 1) % size_x) for i in range(size_x)]
    )
    send, acc, state = merge(acc, state, got, ext)

    def pairs(first, got_row, after):
        (out,) = call(
            functools.partial(pair_kernel, first), "pairs",
            [pair_blocks, ext, got_row, rbf_mix], [((cols, atoms, channels), f32)],
            [
                ((rows + 1, width, atoms + FRAC_ROWS, channels), bf16),
                (((rows + 1) * width, 8, atoms), f32),
                ((2, nrbf * atoms, npb * atoms), bf16),
                ((2, npb * atoms, channels), bf16),
            ],
            smem=1, after=after, us=4.0,
        )
        return out

    messages = [None, None]
    for t in range(2, len(masks)):
        got = cross(send, t)
        after = state
        if t < 4:
            after = messages[t - 2] = pairs(t == 2, got_1 if t == 2 else got_2, state)
        if t < len(masks) - 1:
            send, acc, state = merge(acc, state, got, after)
    (mine,) = merge(acc, state, got, after, last=True)
    theirs = exchange(mine, lambda i: core_bit)

    out = ((cells, atoms, channels), f32)
    (part,) = call(
        own_field_kernel, "own_field", [mine, weight, charge_t, table_mine, embedded, *messages], [out]
    )
    (updated,) = call(
        other_field_kernel, "other_field", [theirs, weight, charge_t, table_theirs, part], [out],
        [out, pltpu.SemaphoreType.DMA((cells,))], out_space=pl.ANY,
    )
    return updated.reshape(embed.shape)


def solution(mesh):
    in_specs = (
        P("gx", "gy", None, None),
        P("gx", "gy", None, None),
        P("gx", "gy", None),
        P(),
        P(),
        P(),
        P(),
        P(),
    )
    out_specs = P("gx", "gy", None, None)
    return jax.shard_map(shards, mesh=mesh, in_specs=in_specs, out_specs=out_specs, check_vma=False)
```

```python
import functools
import math

import jax
import jax.numpy as jnp
from jax import lax
from jax.experimental import pallas as pl
from jax.experimental.pallas import tpu as pltpu
from jax.sharding import PartitionSpec as P

CELL = 5.0
HEIGHT = 51.2
MSG_SCALE = 0.5
LANES = 128
FRAC_ROWS = 16
TAIL = 32
MIB = 1024 * 1024

COS_POLY = (0.9999992251396179, -19.738981246948242, 64.92865753173828, -85.27162170410156, 58.79049301147461, -21.07110595703125)
SIN_POLY = (6.283185005187988, -41.341590881347656, 81.59994506835938, -76.61447143554688, 41.3428840637207, -12.471243858337402)
ENV_POLY = (0.9999998211860657, -0.23369461297988892, 0.019939105957746506, -0.000846334092784673)


def horner(coefs, s):
    acc = coefs[-1] * s + coefs[-2]
    for c in coefs[-3::-1]:
        acc = acc * s + c
    return acc


def pieces(x):
    hi = x.astype(jnp.bfloat16).astype(jnp.float32)
    rest = x - hi
    mid = rest.astype(jnp.bfloat16).astype(jnp.float32)
    return hi, mid, rest - mid


def stack(rows, order):
    row = lax.broadcasted_iota(jnp.int32, (16, LANES), 0)
    out = jnp.zeros((16, LANES), jnp.float32)
    for at, which in enumerate(order):
        out = jnp.where(row == at, jnp.broadcast_to(rows[which], (16, LANES)), out)
    return out.astype(jnp.bfloat16)


def outer_row(column, row):
    return lax.dot_general(
        stack(column, (0, 0, 0, 1, 1, 2)), row, (((0,), (0,)), ((), ())), preferred_element_type=jnp.float32
    )


def row_stack(row):
    return stack(pieces(row), (0, 1, 2, 0, 1, 0))


def put_message(send_ref, half, state):
    parts = [*pieces(state), jnp.zeros_like(state)]
    send_ref[half : half + TAIL, :] = jnp.concatenate(parts, axis=0).astype(jnp.bfloat16)


def half_table(half, k16, x16, sums_rhs, mean, state_ref, table_ref, store):
    kvec = table_ref.shape[0]
    nb = kvec // LANES
    offset = half.astype(jnp.float32) * 0.25
    lane = lax.broadcasted_iota(jnp.int32, (LANES, LANES), 1)
    counts = jnp.zeros((LANES, LANES), jnp.float32)
    for b in range(nb):
        at = slice(b * LANES, (b + 1) * LANES)
        turns = lax.dot_general(k16[:, at], x16, (((0,), (0,)), ((), ())), preferred_element_type=jnp.float32)
        turns = turns - offset
        turns = turns - jnp.round(turns)
        table = horner(COS_POLY, turns * turns).astype(jnp.bfloat16)
        table_ref[at, :] = table
        total = jnp.dot(table, sums_rhs(), preferred_element_type=jnp.float32)
        count = total[:, LANES:]
        counts = jnp.where(lane == b, count, counts)
        store(at, total[:, :LANES] - count * mean)
    row = lax.broadcasted_iota(jnp.int32, (8, LANES), 0)
    state_ref[...] = jnp.where(row == nb, jnp.broadcast_to(mean, (8, LANES)), jnp.transpose(counts)[0:8])


def sent_kernel(
    nx, ny, frac_hbm, kidx_hbm, emb_hbm, in_hbm, charge_hbm, weight_hbm,
    table_ref, send_ref, k16_ref, x16_ref, rhs, mean_ref, frac_ref, in_ref, charge_ref, weight_ref,
    kf32, xf32, state, kidx_ref, sems,
):
    rows, _, cols, atoms = frac_ref.shape
    kvec = kidx_ref.shape[1]
    n = rows * cols * atoms
    fetches = [
        pltpu.make_async_copy(kidx_hbm, kidx_ref, sems.at[0]),
        pltpu.make_async_copy(frac_hbm, frac_ref, sems.at[1]),
        pltpu.make_async_copy(emb_hbm, rhs.at[:, 0:LANES], sems.at[2]),
        pltpu.make_async_copy(in_hbm, in_ref, sems.at[3]),
        pltpu.make_async_copy(charge_hbm, charge_ref, sems.at[4]),
        pltpu.make_async_copy(weight_hbm, weight_ref, sems.at[5]),
    ]
    for fetch in fetches:
        fetch.start()
    me_x, me_y = lax.axis_index("gx"), lax.axis_index("gy")
    kf32[...] = jnp.zeros_like(kf32)
    xf32[...] = jnp.zeros_like(xf32)
    rhs[:, LANES:] = jnp.ones((n, LANES), jnp.bfloat16)
    fetches[0].wait()
    fetches[1].wait()
    kf = kidx_ref[...].astype(jnp.float32)
    kf32[0:1, :] = kf[0:1] * (1.0 / nx)
    kf32[1:2, :] = kf[0:1] * (1.0 / nx)
    kf32[2:3, :] = kf[1:2] * (1.0 / ny)
    kf32[3:4, :] = kf[1:2] * (1.0 / ny)
    kf32[4:5, :] = kf[2:3]
    for r in range(rows):
        f = [frac_ref[r, q].astype(jnp.float32) for q in range(3)]
        for c in range(cols):
            at = slice((r * cols + c) * atoms, (r * cols + c + 1) * atoms)
            xf32[0:1, at] = jnp.full((1, atoms), me_x * rows + r, jnp.int32).astype(jnp.float32)
            xf32[1:2, at] = f[0][c : c + 1]
            xf32[2:3, at] = jnp.full((1, atoms), me_y * cols + c, jnp.int32).astype(jnp.float32)
            xf32[3:4, at] = f[1][c : c + 1]
            xf32[4:5, at] = f[2][c : c + 1]
    k16 = kf32[...].astype(jnp.bfloat16)
    x16 = xf32[...].astype(jnp.bfloat16)
    k16_ref[...] = k16
    x16_ref[...] = x16
    fetches[2].wait()
    mean = jnp.sum(rhs[:, 0:LANES].astype(jnp.float32), axis=0, keepdims=True) * (1.0 / n)
    mean_ref[...] = jnp.broadcast_to(mean, mean_ref.shape)

    def store(at, centred):
        send_ref[at, :] = centred.astype(jnp.bfloat16)

    half_table(1 - lax.rem(me_x, 2), k16, x16, lambda: rhs[...], mean, state, table_ref, store)
    put_message(send_ref, kvec, state[...])
    for fetch in fetches[3:]:
        fetch.wait()


def kept_kernel(k16_ref, x16_ref, rhs_ref, mean_ref, table_ref, acc_ref, state_ref):
    def store(at, centred):
        acc_ref[at, :] = centred

    core = lax.rem(lax.axis_index("gx"), 2)
    half_table(
        core, k16_ref[...], x16_ref[...], lambda: rhs_ref[...], mean_ref[0:1], state_ref, table_ref, store
    )


def merge_kernel(last, acc_ref, state_ref, got_ref, after_ref, *outs):
    del after_ref
    half = acc_ref.shape[0]
    nb = half // LANES
    tail = got_ref[half : half + TAIL, :].astype(jnp.float32)
    theirs = tail[0:8] + tail[8:16] + tail[16:24]
    mine = state_ref[...]
    weight = jnp.where(lax.broadcasted_iota(jnp.int32, (8, LANES), 0) < nb, 1.0, 0.5)
    state = (mine + theirs) * weight
    diff = (mine - theirs) * weight
    split = pieces(diff)
    means = row_stack(diff[nb : nb + 1])
    for b in range(nb):
        at = slice(b * LANES, (b + 1) * LANES)
        part = outer_row([piece[b : b + 1] for piece in split], means)
        merged = acc_ref[at, :] + got_ref[at, :].astype(jnp.float32) + part
        if not last:
            outs[1][at, :] = merged
        outs[0][at, :] = merged.astype(jnp.bfloat16)
    if not last:
        outs[2][...] = state
        put_message(outs[0], half, state)


def feats_kernel(scale, frac_ref, emb_ref, w_ref, charge_ref, weight_ref, after_ref, out_ref, charge_t_ref, scaled_ref):
    del after_ref
    rows, parts, cols, atoms = frac_ref.shape
    feats = jnp.dot(emb_ref[:, 0:LANES], w_ref[...], preferred_element_type=jnp.float32).astype(jnp.bfloat16)
    row = lax.broadcasted_iota(jnp.int32, (FRAC_ROWS, atoms), 0)
    for r in range(rows):
        f = [frac_ref[r, q].astype(jnp.float32) for q in range(parts)]
        for c in range(cols):
            at = (r * cols + c) * atoms
            out_ref[r, c, 0:atoms, :] = feats[at : at + atoms]
            packed = jnp.zeros((FRAC_ROWS, atoms), jnp.float32)
            for q in range(parts):
                packed = jnp.where(row == q, jnp.broadcast_to(f[q][c : c + 1], (FRAC_ROWS, atoms)), packed)
            out_ref[r, c, atoms : atoms + FRAC_ROWS, :] = packed.astype(jnp.bfloat16)
    charge_t_ref[...] = jnp.transpose(charge_ref[...].astype(jnp.float32)).astype(jnp.bfloat16)
    scaled_ref[...] = weight_ref[...] * scale


def pair_kernel(first, codes_ref, ext_ref, got_ref, mix_ref, after_ref, out_ref, near3, fields, basis, gathered):
    del after_ref
    rows, width, packed, channels = ext_ref.shape
    atoms = packed - FRAC_ROWS
    cols = width - 2
    npb = codes_ref.shape[-1]
    nrbf = mix_ref.shape[0]
    core = lax.rem(lax.axis_index("gx"), 2)
    above = core if first else 1 - core
    row = 1 - above

    @pl.when(above == 0)
    def _():
        near3[0:rows] = ext_ref[...]
        near3[rows] = got_ref[...]

    @pl.when(above == 1)
    def _():
        near3[0] = got_ref[...]
        near3[1 : rows + 1] = ext_ref[...]

    for r in range(rows + 1):
        for c in range(width):
            fields[r * width + c] = near3[r, c, atoms:packed, :].astype(jnp.float32)[0:8]

    order = lax.broadcasted_iota(jnp.int32, (nrbf, channels), 0).astype(jnp.float32) - nrbf // 2
    mix = mix_ref[...] * (jnp.exp(-order * order) * MSG_SCALE)
    bits = math.sqrt(math.log2(math.e))

    for c in range(cols):
        own = fields[width + c + 1]
        own = jnp.transpose(jnp.concatenate([own] * (LANES // 8), axis=0))
        own_x = jnp.broadcast_to(own[:, 0:1], (atoms, atoms))
        own_y = jnp.broadcast_to(own[:, 1:2], (atoms, atoms))
        own_z = jnp.broadcast_to(own[:, 2:3] * (HEIGHT / CELL), (atoms, atoms))
        slot = c % 2
        for p in range(npb):
            code = codes_ref[row, c, p]
            step_x, step_y = code // 3 - 1, code % 3 - 1
            near = fields[(1 + step_x) * width + c + 1 + step_y]
            dx = (near[0:1] + step_x.astype(jnp.float32)) - own_x
            dy = (near[1:2] + step_y.astype(jnp.float32)) - own_y
            dz = jnp.abs(near[2:3] * (HEIGHT / CELL) - own_z)
            dz = jnp.minimum(dz, HEIGHT / CELL - dz)
            s = jnp.minimum(dx * dx + dy * dy + dz * dz, 1.0)
            root = s * lax.rsqrt(jnp.maximum(s, 1e-30))
            z = root * (bits * (nrbf - 1)) - bits * (nrbf // 2)
            env = (1.0 - s) * horner(ENV_POLY, s)
            mid = env * env * jnp.exp2(-(z * z))
            up, down = jnp.exp2((2.0 * bits) * z), jnp.exp2((-2.0 * bits) * z)
            at = slice(p * atoms, (p + 1) * atoms)
            value = mid
            for q in range(nrbf // 2, nrbf):
                basis[slot, q * atoms : (q + 1) * atoms, at] = value.astype(jnp.bfloat16)
                value = value * up
            value = mid
            for q in range(nrbf // 2 - 1, -1, -1):
                value = value * down
                basis[slot, q * atoms : (q + 1) * atoms, at] = value.astype(jnp.bfloat16)
            gathered[slot, at, :] = near3[1 + step_x, c + 1 + step_y, 0:atoms, :]
        parts = jnp.dot(basis[slot], gathered[slot], preferred_element_type=jnp.float32)
        total = parts[0:atoms] * mix[0:1]
        for q in range(1, nrbf):
            total = total + parts[q * atoms : (q + 1) * atoms] * mix[q : q + 1]
        out_ref[c] = total


def field_factors(half_ref, weight_ref, charge_t_ref):
    factors = lax.dot_general(
        charge_t_ref[...], half_ref[...], (((1,), (1,)), ((), ())), preferred_element_type=jnp.float32
    )
    return (factors * weight_ref[...]).astype(jnp.bfloat16)


def own_field_kernel(half_ref, weight_ref, charge_t_ref, table_ref, emb_ref, msg1_ref, msg2_ref, out_ref):
    cols, atoms, _ = msg1_ref.shape
    row1 = 1 - lax.rem(lax.axis_index("gx"), 2)
    factors = field_factors(half_ref, weight_ref, charge_t_ref)
    total = jnp.dot(factors, table_ref[...], preferred_element_type=jnp.float32)
    for r in range(2):
        for c in range(cols):
            i = r * cols + c
            at = slice(i * atoms, (i + 1) * atoms)
            msg = jnp.where(row1 == r, msg1_ref[c], msg2_ref[c])
            out_ref[i] = emb_ref[at, 0:LANES].astype(jnp.float32) + msg + jnp.transpose(total[:, at])


def other_field_kernel(half_ref, weight_ref, charge_t_ref, table_ref, part_ref, out_ref, done, sems):
    cells, atoms, _ = done.shape
    factors = field_factors(half_ref, weight_ref, charge_t_ref)
    copies = []
    for i in range(cells):
        if i % 2 == 0:
            at = slice(i * atoms, (i + 2) * atoms)
            total = jnp.dot(factors, table_ref[:, at], preferred_element_type=jnp.float32)
        done[i] = part_ref[i] + jnp.transpose(total[:, (i % 2) * atoms : (i % 2 + 1) * atoms])
        copy = pltpu.make_async_copy(done.at[i], out_ref.at[i], sems.at[i])
        copy.start()
        copies.append(copy)
    for copy in copies:
        copy.wait()


def in_hbm(x):
    return pltpu.with_memory_space_constraint(x, pltpu.HBM)


def vmem(count):
    return [pl.BlockSpec(memory_space=pltpu.VMEM)] * count


def shards(embed, frac, pair_blocks, w_in, rbf_mix, w_charge, k_index, k_weight):
    f32, bf16 = jnp.float32, jnp.bfloat16
    rows, cols, atoms, channels = embed.shape
    kvec = k_weight.shape[0]
    npb = pair_blocks.shape[-1]
    nrbf = rbf_mix.shape[0]
    size_x, size_y = lax.axis_size("gx"), lax.axis_size("gy")
    count = size_x * size_y
    cells = rows * cols
    width = cols + 2
    unread = [pl.BlockSpec(memory_space=pl.ANY)]

    def call(body, name, ins, outs, scratch=(), smem=0, after=None, us=1.0, out_space=pltpu.VMEM, hbm=0):
        specs = [pl.BlockSpec(memory_space=pltpu.SMEM)] * smem + vmem(len(ins) - smem - hbm)
        specs += [pl.BlockSpec(memory_space=pltpu.HBM)] * hbm
        if after is not None:
            ins, specs = [*ins, after], specs + unread
        return pl.pallas_call(
            body,
            out_shape=[jax.ShapeDtypeStruct(*o) for o in outs],
            in_specs=specs,
            out_specs=[pl.BlockSpec(memory_space=out_space)] * len(outs),
            scratch_shapes=[pltpu.VMEM(*s) if isinstance(s, tuple) else s for s in scratch],
            compiler_params=pltpu.CompilerParams(vmem_limit_bytes=32 * MIB),
            cost_estimate=pl.CostEstimate(flops=int(us * 1.15e9), bytes_accessed=0, transcendentals=0),
            name=name,
        )(*ins)

    def exchange(values, mask_of):
        return lax.ppermute(values, ("gx", "gy"), [(i, i ^ mask_of(i)) for i in range(count)])

    acc_out, state_out = ((kvec, channels), f32), ((8, LANES), f32)
    send_out = ((kvec + TAIL, channels), bf16)
    table_out = ((kvec, cells * atoms), bf16)
    k16, x16 = (16, kvec), (16, cells * atoms)
    table_theirs, send, k16_in, x16_in, embedded, mean, parts, w_near, charge_near, weight_near = call(
        functools.partial(sent_kernel, rows * size_x, cols * size_y), "sent_half",
        [
            in_hbm(x)
            for x in (
                jnp.transpose(frac, (0, 2, 1, 3)), k_index, embed.reshape(-1, channels), w_in, w_charge,
                k_weight.reshape(1, kvec),
            )
        ],
        [table_out, send_out, (k16, bf16), (x16, bf16), ((cells * atoms, 2 * LANES), bf16), state_out,
         ((rows, frac.shape[2], cols, atoms), bf16), (w_in.shape, bf16), (w_charge.shape, bf16), ((1, kvec), f32)],
        [(k16, f32), (x16, f32), state_out, (k_index.shape, jnp.int32), pltpu.SemaphoreType.DMA((6,))],
        hbm=6, us=2.5,
    )

    table_mine, acc, state = call(
        kept_kernel, "kept_half", [k16_in, x16_in, embedded, mean], [table_out, acc_out, state_out], us=2.5
    )

    def merge(acc, state, got, after, last=False):
        outs = [((kvec, channels), bf16)] if last else [send_out, acc_out, state_out]
        return call(functools.partial(merge_kernel, last), "merge", [acc, state, got], outs, after=after, us=5.0)

    core_bit = size_y
    along_y = [1 << b for b in range(size_y.bit_length() - 1)]
    along_x = [core_bit << b for b in range(1, size_x.bit_length() - 1)]
    masks = [along_x[0], *along_y, *along_x[:0:-1]]
    swapped = [*along_x[1:], along_x[0], *along_y]

    def cross(send, t):
        return exchange(send, lambda i: swapped[t] if i & core_bit else masks[t])

    send, acc, state = merge(acc, state, exchange(send, lambda i: core_bit), table_mine)

    got = cross(send, 0)
    packed, charge_t, weight = call(
        functools.partial(feats_kernel, 1.0 / math.sqrt(cells * count * atoms * kvec)), "feats",
        [parts, embedded, w_near, charge_near, weight_near],
        [((rows, cols, atoms + FRAC_ROWS, channels), bf16), (w_charge.shape, bf16), ((1, kvec), f32)], after=state,
    )
    if size_y == 2:
        edges = lax.ppermute(jnp.stack([packed[:, -1], packed[:, 0]], axis=1), "gy", [(0, 1), (1, 0)])
        west, east = edges[:, 0:1], edges[:, 1:2]
    else:
        west = lax.ppermute(packed[:, -1:], "gy", [(i, (i + 1) % size_y) for i in range(size_y)])
        east = lax.ppermute(packed[:, :1], "gy", [((i + 1) % size_y, i) for i in range(size_y)])
    send, acc, state = merge(acc, state, got, packed)

    got = cross(send, 1)
    ext = jnp.concatenate([west, packed, east], axis=1)
    core = lax.rem(lax.axis_index("gx"), 2)
    toward_1 = lax.dynamic_index_in_dim(ext, 1 - core, 0, keepdims=False)
    toward_2 = lax.dynamic_index_in_dim(ext, core, 0, keepdims=False)
    got_1 = lax.ppermute(toward_1, "gx", [(i, i ^ 1) for i in range(size_x)])
    got_2 = lax.ppermute(
        toward_2, "gx", [(i, (i - 1) % size_x if i % 2 == 0 else (i + 1) % size_x) for i in range(size_x)]
    )
    send, acc, state = merge(acc, state, got, ext)

    def pairs(first, got_row, after):
        (out,) = call(
            functools.partial(pair_kernel, first), "pairs",
            [pair_blocks, ext, got_row, rbf_mix], [((cols, atoms, channels), f32)],
            [
                ((rows + 1, width, atoms + FRAC_ROWS, channels), bf16),
                (((rows + 1) * width, 8, atoms), f32),
                ((2, nrbf * atoms, npb * atoms), bf16),
                ((2, npb * atoms, channels), bf16),
            ],
            smem=1, after=after, us=4.0,
        )
        return out

    messages = [None, None]
    for t in range(2, len(masks)):
        got = cross(send, t)
        after = state
        if t < 4:
            after = messages[t - 2] = pairs(t == 2, got_1 if t == 2 else got_2, state)
        if t < len(masks) - 1:
            send, acc, state = merge(acc, state, got, after)
    (mine,) = merge(acc, state, got, after, last=True)
    theirs = exchange(mine, lambda i: core_bit)

    out = ((cells, atoms, channels), f32)
    (part,) = call(
        own_field_kernel, "own_field", [mine, weight, charge_t, table_mine, embedded, *messages], [out]
    )
    (updated,) = call(
        other_field_kernel, "other_field", [theirs, weight, charge_t, table_theirs, part], [out],
        [out, pltpu.SemaphoreType.DMA((cells,))], out_space=pl.ANY,
    )
    return updated.reshape(embed.shape)


def solution(mesh):
    in_specs = (
        P("gx", "gy", None, None),
        P("gx", "gy", None, None),
        P("gx", "gy", None),
        P(),
        P(),
        P(),
        P(),
        P(),
    )
    out_specs = P("gx", "gy", None, None)
    return jax.shard_map(shards, mesh=mesh, in_specs=in_specs, out_specs=out_specs, check_vma=False)
```
